512 devices in a mesh: seq: 64 (over z_hi, y, core), head: 8 (over z_lo, x).
Axes of the slice: x: 4, y: 8, z: 8 (z_hi: 4, z_lo: 2; z = z_hi * 2 + z_lo), core: 2. Of those that a mesh axis runs over, the one named last changes fastest.
Arguments:
- query_feats: bfloat16 [32768, 4096], P('seq', 'head'), may hold values from -16 to 16
- key_feats: bfloat16 [32768, 1024], P('seq', 'head'), may hold values from -7 to 7
- value_feats: bfloat16 [32768, 1024], P('seq', 'head'), may hold values from -6 to 6
- span_class: int32 [32], replicated, may hold values from 1 to 16, as said below
- ramp_width: int32 [32], replicated, may hold values from 32 to 128
- doc_lengths: int32 [16], replicated, may hold values from 1 to 16384, 32768 in all
- out_proj: bfloat16 [4096, 4096], P('seq', 'head'), may hold values from -0.5 to 0.5
Outputs:
- mixed: bfloat16 [32768, 4096], P(('seq', 'head'))
The draws below stay inside these ranges and needn't reach their ends.
Inputs may be any that keep to these rules, and one draw needn't show every extreme that they name: `span_class`: some head has a span of 16 tiles.
All inputs are finite; a program needn't handle non-finite values.
Results may differ from the reference program's by a relative error of at most 0.014.
Values may be sent and summed in bfloat16 or wider, within the bound.
A program may use at most 64 MiB of HBM per device.

```python
import math
import jax
import jax.numpy as jnp
import numpy as np
from jax import lax

D = 4096
H = 32
KVH = 8
HD = 128
TOK_DEV = 512
TILE = 128
MAXBLK = 16
BACK = 4
GROUP_HEADS = 4
TOKENS = 32768
NDOCS = 16
N_SEQ = 64
N_HEAD = 8


def draw_query_feats(key, part):
    result = jnp.clip(1.5 * jax.random.normal(jax.random.fold_in(key, 21), (TOKENS, H * HD), jnp.float32), -6.0, 6.0)
    return result.astype(jnp.bfloat16)


def draw_key_feats(key, part):
    result = jnp.clip(jax.random.normal(jax.random.fold_in(key, 31), (TOKENS, KVH * HD), jnp.float32), -4.0, 4.0)
    return result.astype(jnp.bfloat16)


def draw_span_class(key, part):
    first_draw = jax.random.randint(jax.random.fold_in(key, 41), (H,), 1, MAXBLK + 1)
    second_draw = jax.random.randint(jax.random.fold_in(key, 42), (H,), 1, MAXBLK + 1)
    skewed = jnp.maximum(first_draw * second_draw // MAXBLK, 1)
    longest = jax.random.randint(jax.random.fold_in(key, 43), (), 0, H)
    return jnp.where(jnp.arange(H, dtype=jnp.int32) == longest, MAXBLK, skewed).astype(jnp.int32)


def place_ends(entries, key, least, top_value):
    shape = entries.shape
    spot = [jax.random.randint(jax.random.fold_in(key, axis), (), 0, shape[axis]) for axis in range(len(shape))]
    entries = entries.at[tuple(spot)].set(least)
    longest = shape.index(max(shape))
    spot[longest] = (spot[longest] + 1) % shape[longest]
    return entries.at[tuple(spot)].set(top_value)


def block_scale(rng, extent, pieces, least, high):
    def one(dim, shards_of):
        heights = jax.random.uniform(jax.random.fold_in(jax.random.fold_in(rng, 6), dim), (shards_of,), jnp.float32, least / len(pieces), high / len(pieces))
        return jnp.repeat(jnp.exp(heights), extent[dim] // shards_of).reshape((-1,) + (1,) * (len(extent) - dim - 1))

    gain = one(*pieces[0])
    for cut in pieces[1:]:
        gain = gain * one(*cut)
    return gain


def split_up(number_of, total, most, slope):
    loads = [(1 << 20) // math.isqrt(grade ** slope) + 1 for grade in range(2, number_of + 1)]
    spare, holding = total - most - (number_of - 1), [1] * (number_of - 1)
    while spare > 0:
        free = [i for i in range(number_of - 1) if holding[i] < most]
        whole, budget = sum([loads[i] for i in free]), spare
        for i in free:
            extra = min(most - holding[i], max(1, budget * loads[i] // whole), spare)
            holding[i] = holding[i] + extra
            spare = spare - extra
    return np.array([most] + holding)


def uneven_parts(key, count, total, most, slope):
    if count == 2:
        one = jax.random.randint(key, (), max(1, total - most), min(most, total - 1) + 1)
        return jnp.stack([one, total - one])
    lengths = jnp.asarray(split_up(count, total, most, slope), jnp.int32)
    couples = (count - 1) // 2
    source_of, taker = lengths[1:1 + 2 * couples:2], lengths[2:2 + 2 * couples:2]
    room = jnp.minimum(source_of - 1, most - taker)
    shifted = jax.random.randint(jax.random.fold_in(key, 1), (couples,), 0, 1 << 20) % (room + 1)
    lengths = lengths.at[1:1 + 2 * couples:2].set(source_of - shifted).at[2:2 + 2 * couples:2].set(taker + shifted)
    return lengths[jax.random.permutation(jax.random.fold_in(key, 2), count)]


def scatter_about(key, dims, width, reach, cuts=(), kind=jnp.bfloat16):
    array = jax.random.normal(key, dims, jnp.float32) * width
    if len(cuts) > 0:
        array = block_scale(key, dims, cuts, -0.22, 0.18) * array
    return jnp.clip(array, min=-reach, max=reach).astype(kind)


def setup_inputs(seed: int = 0) -> dict:
    key_of = jax.random.split(jax.random.key(seed), 8)
    query_feats = draw_query_feats(jax.random.fold_in(key_of[7], 71), 0)
    key_feats = draw_key_feats(jax.random.fold_in(key_of[7], 71), 0)
    value_feats = scatter_about(key_of[2], (TOKENS, KVH * HD), 1.0, 6.0, ((0, 64), (1, 8)))
    span_class = draw_span_class(jax.random.fold_in(key_of[7], 71), 0)
    ramp_width = place_ends(jax.random.randint(key_of[4], (H,), TILE // 4, TILE + 1), jax.random.fold_in(key_of[4], 1), TILE // 4, TILE).astype(jnp.int32)
    doc_lengths = uneven_parts(key_of[5], NDOCS, TOKENS, TOKENS // 2, 2).astype(jnp.int32)
    out_proj = scatter_about(key_of[6], (D, H * HD), HD ** -0.5, 0.5, ((0, 64), (1, 8)))
    return dict(query_feats=query_feats, key_feats=key_feats, value_feats=value_feats, span_class=span_class, ramp_width=ramp_width, doc_lengths=doc_lengths, out_proj=out_proj)


very_low = -1e+30

def reference(query_feats, key_feats, value_feats, span_class, ramp_width, doc_lengths, out_proj):
    window = (BACK + 1) * TOK_DEV
    group_width = GROUP_HEADS * HD
    ratio = H // KVH
    starts = jnp.cumsum(doc_lengths) - doc_lengths
    span_end = (span_class * TILE).astype(jnp.float32)
    ramp_float = ramp_width.astype(jnp.float32)
    pad_rows = jnp.zeros((BACK * TOK_DEV, KVH * HD), key_feats.dtype)
    key_pad = jnp.concatenate([pad_rows, key_feats], axis=0)
    value_pad = jnp.concatenate([pad_rows, value_feats], axis=0)

    def one_block(block):
        first = (block * TOK_DEV).astype(jnp.int32)
        query_pos = first + jnp.arange(TOK_DEV, dtype=jnp.int32)
        key_pos = first - BACK * TOK_DEV + jnp.arange(window, dtype=jnp.int32)
        doc_start = lax.optimization_barrier(jnp.max(jnp.where(starts[None, :] <= query_pos[:, None], starts[None, :], 0), axis=1))
        query_blk = lax.dynamic_slice_in_dim(query_feats, first, TOK_DEV, 0).reshape(TOK_DEV, H, HD).astype(jnp.float32)
        key_blk = lax.dynamic_slice_in_dim(key_pad, first, window, 0).reshape(window, KVH, HD).astype(jnp.float32)
        value_blk = lax.dynamic_slice_in_dim(value_pad, first, window, 0).reshape(window, KVH, HD).astype(jnp.float32)
        key_blk = jnp.repeat(key_blk, ratio, axis=1)
        value_blk = jnp.repeat(value_blk, ratio, axis=1)
        scores = jnp.einsum('qhd,khd->qhk', query_blk, key_blk, precision=lax.Precision.HIGHEST) * (1.0 / math.sqrt(HD))
        distance = query_pos[:, None] - key_pos[None, :]
        visible = (distance >= 0) & (key_pos[None, :] >= doc_start[:, None])
        weights = jnp.clip((span_end[None, :, None] - distance[:, None, :].astype(jnp.float32)) / ramp_float[None, :, None], 0.0, 1.0)
        weights = jnp.where(visible[:, None, :], weights, 0.0)
        limited = jnp.where(weights > 0.0, scores, very_low)
        top_score = lax.optimization_barrier(jnp.max(limited, axis=2))
        prob_terms = weights * jnp.exp(limited - top_score[:, :, None])
        denominator = lax.optimization_barrier(jnp.sum(prob_terms, axis=2))
        rounded = lax.optimization_barrier(prob_terms.astype(jnp.bfloat16)).astype(jnp.float32)
        numerator = jnp.einsum('qhk,khd->qhd', rounded, value_blk, precision=lax.Precision.HIGHEST)
        attended = (numerator / denominator[:, :, None]).astype(jnp.bfloat16).reshape(TOK_DEV, H * HD)
        mixed_sum = jnp.zeros((TOK_DEV, D), jnp.float32)
        for group in range(N_HEAD):
            low_col = group * group_width
            part_out = jnp.dot(attended[:, low_col:low_col + group_width], out_proj[:, low_col:low_col + group_width].T, preferred_element_type=jnp.float32)
            mixed_sum = mixed_sum + lax.optimization_barrier(part_out.astype(jnp.bfloat16)).astype(jnp.float32)
        return mixed_sum.astype(jnp.bfloat16)
    blocks = lax.map(one_block, jnp.arange(N_SEQ, dtype=jnp.int32))
    return blocks.reshape(N_SEQ * TOK_DEV, D)
```

```python
import math

import jax
import jax.numpy as jnp
from jax import lax
from jax.experimental import pallas as pl
from jax.experimental.pallas import tpu as pltpu
from jax.sharding import PartitionSpec as P

HD = 128
TILE = 128
HEADS = 4
TOK = 512
FEAT = HEADS * HD
NZ, NY, NX = 4, 8, 4
NDOCS = 16
ROWS = 64
PLUS, MINUS = 3, 4
COLS = 512
LOW = -1e30
MESH = pl.DeviceIdType.MESH
NT = (((1,), (1,)), ((), ()))
SCALE = math.log2(math.e) / math.sqrt(HD)


def kernel(q_ref, k_ref, v_ref, w_ref, span_ref, ramp_ref, doc_ref, out_ref,
           kbuf, vbuf, qx, kf, btab, s_scr, p_scr, m_scr, acc, att, wg, part,
           far, near, zout, zin,
           kv_send, kv_recv, z_send, z_recv, p_send, p_recv, m_send, m_recv,
           s_send, s_recv, a_send, a_recv, far_send, far_recv, near_send, near_recv,
           zx_send, zx_recv):
    seq = lax.axis_index("seq")
    head = lax.axis_index("head")
    core = lax.rem(seq, 2)
    y = lax.rem(seq // 2, NY)
    zh = seq // (2 * NY)
    x = lax.rem(head, NX)
    zl = head // NX
    half = zh // 2
    n_seq = 2 * NY * NZ

    def at(zh_, y_, c_, zl_, x_):
        return ((zh_ * NY + y_) * 2 + c_, zl_ * NX + x_)

    after = (lax.rem(seq + 2, n_seq), head)
    before = (lax.rem(seq + n_seq - 2, n_seq), head)
    sibling = at(zh, y, 1 - core, zl, x)
    y_up = at(zh, lax.rem(y + 1, NY), core, zl, x)
    y_down = at(zh, lax.rem(y + NY - 1, NY), core, zl, x)
    xr, xl = lax.rem(x + 1, NX), lax.rem(x + NX - 1, NX)
    xo = lax.rem(x + 2, NX)
    x_up = at(zh, y, core, zl, xr)
    x_down = at(zh, y, core, zl, xl)
    partner = at(zh, y, core, 1 - zl, x)

    barrier = pltpu.get_barrier_semaphore()
    greet = [after, before, sibling, y_up, y_down, x_up, x_down, partner]
    for j in range(1, NZ):
        for b in range(2):
            greet.append(at(lax.rem(zh + j, NZ), y, core, b, x))
    for device in greet:
        pl.semaphore_signal(barrier, inc=1, device_id=device, device_id_type=MESH)

    lane = lax.broadcasted_iota(jnp.int32, (1, HD), 1)
    starts = jnp.zeros((1, HD), jnp.int32)
    ends = jnp.zeros((1, HD), jnp.int32)
    total = jnp.int32(0)
    for n in range(NDOCS):
        starts = jnp.where(lane == n, total, starts)
        total = total + doc_ref[n]
        ends = jnp.where(lane == n, total, ends)
    row_of = lax.broadcasted_iota(jnp.int32, (TILE, HD), 0)
    lane_of = lax.broadcasted_iota(jnp.int32, (TILE, HD), 1)
    named = lane_of < NDOCS

    def features(n, carry):
        pos = seq * TOK + n * TILE + row_of
        inside = (pos >= starts) & (pos < ends)
        other = jnp.where(named & jnp.logical_not(inside), 1.0, 0.0).astype(jnp.bfloat16)
        for h in range(HEADS):
            qx[n, h * TILE:(h + 1) * TILE, HD:] = other
            qx[n, h * TILE:(h + 1) * TILE, :HD] = q_ref[pl.ds(pl.multiple_of(n * TILE, TILE), TILE), h * HD:(h + 1) * HD]
        for d in range(5):
            key_pos = pos - d * TOK
            hidden = ((key_pos >= starts) & (key_pos < ends)) | (key_pos < 0)
            kf[d, pl.ds(pl.multiple_of(n * TILE, TILE), TILE), :] = jnp.where(named & hidden, LOW, 0.0).astype(jnp.bfloat16)
        return carry

    lax.fori_loop(0, TOK // TILE, features, 0)

    diff = (row_of - lane_of).astype(jnp.float32)

    def weight(distance_left, ramp, seen):
        w = jnp.clip(distance_left / ramp, 0.0, 1.0)
        keep = (w > 0.0) & seen
        return jnp.where(keep, jnp.log2(jnp.where(keep, w, 1.0)), LOW)

    for h in range(HEADS):
        ramp = ramp_ref[head * HEADS + h].astype(jnp.float32)
        span = span_ref[head * HEADS + h].astype(jnp.float32) * float(TILE)
        always = diff < 1000.0
        btab[h, 0] = jnp.zeros((TILE, HD), jnp.float32)
        btab[h, 1] = weight(float(TILE) - diff, ramp, always)
        btab[h, 2] = weight(-diff, ramp, always)
        btab[h, 3] = weight(span - diff, ramp, diff >= 0.0)
        btab[h, 4] = jnp.full((TILE, HD), LOW, jnp.float32)

    pl.semaphore_wait(barrier, len(greet))

    def remote(src, dst, send, recv, device):
        return pltpu.make_async_remote_copy(
            src_ref=src, dst_ref=dst, send_sem=send, recv_sem=recv,
            device_id=device, device_id_type=MESH)

    def kv_copies(k_src, v_src, slot, n, device):
        return (remote(k_src, kbuf.at[slot], kv_send.at[n, 0], kv_recv.at[slot, 0], device),
                remote(v_src, vbuf.at[slot], kv_send.at[n, 1], kv_recv.at[slot, 1], device))

    def start(copies):
        for c in copies:
            c.start()

    def kv_arrived(slot):
        for c in kv_copies(k_ref, v_ref, slot, 0, sibling):
            c.wait_recv()

    start(kv_copies(k_ref, v_ref, 1, 0, after))

    @pl.when(core == 0)
    def _():
        start(kv_copies(k_ref, v_ref, 0, 2, sibling))

    mine = (zl, lax.rem(zh, 2))

    def z_copy(j):
        target = at(lax.rem(zh + j, NZ), y, core, half, x)
        return remote(w_ref, wg.at[mine[0], mine[1], y, core], z_send.at[j], z_recv.at[mine[0], mine[1]], target)

    for j in range(1, NZ):
        z_copy(j).start()

    @pl.when(half == zl)
    def _():
        pltpu.make_async_copy(w_ref, wg.at[mine[0], mine[1], y, core], z_recv.at[mine[0], mine[1]]).start()

    @pl.when(half != zl)
    def _():
        z_copy(0).start()

    def chunk(y_, c_):
        return wg.at[:, :, y_, c_]

    def ring_up(n):
        src = chunk(lax.rem(y + NY - n, NY), core)
        return remote(src, src, p_send.at[n], p_recv.at[n], y_up)

    def ring_down(n):
        src = chunk(lax.rem(y + n, NY), core)
        return remote(src, src, m_send.at[n], m_recv.at[n], y_down)

    def got_up(n):
        src = chunk(lax.rem(y + NY - n - 1, NY), core)
        return remote(src, src, p_send.at[n], p_recv.at[n], y_up)

    def got_down(n):
        src = chunk(lax.rem(y + n + 1, NY), core)
        return remote(src, src, m_send.at[n], m_recv.at[n], y_down)

    def share(n):
        src = chunk(lax.rem(y + n, NY), core)
        return remote(src, src, s_send.at[n], s_recv.at[n], sibling)

    def shared(n):
        src = chunk(lax.rem(y + n, NY), 1 - core)
        return remote(src, src, s_send.at[n], s_recv.at[n], sibling)

    def ring_begin():
        for a in range(2):
            for b in range(2):
                dst = wg.at[a, b, y, core]
                remote(w_ref, dst, z_send.at[0], z_recv.at[a, b], sibling).wait_recv()
        ring_down(0).start()
        ring_up(0).start()
        share(0).start()

    def ring_step(n):
        if n < MINUS:
            got_down(n).wait_recv()
            if n + 1 < MINUS:
                ring_down(n + 1).start()
            share(n + 1).start()
        if n < PLUS:
            got_up(n).wait_recv()
            if n + 1 < PLUS:
                ring_up(n + 1).start()
            share(NY - n - 1).start()

    def send_att(i):
        rows = att.at[zl, pl.ds(pl.multiple_of(i * TILE, TILE), TILE)]
        return remote(rows, rows, a_send.at[i], a_recv.at[i], partner)

    def attend(d, keys, values, last=False):
        def tile(i, carry):
            kx = jnp.concatenate([keys[...], kf[d]], axis=1)
            s_scr[...] = lax.dot_general(qx[i], kx, NT, preferred_element_type=jnp.float32)
            for h in range(HEADS):
                span = span_ref[head * HEADS + h]
                rows = slice(h * TILE, (h + 1) * TILE)
                terms = []
                for t in range(4):
                    delta = 4 * d + i - t
                    over = delta - span
                    table = jnp.where(over > 0, 4, jnp.maximum(over + 2, 0))
                    table = jnp.where(delta > 0, table, jnp.where(delta == 0, 3, 4))
                    terms.append(s_scr[rows, t * TILE:(t + 1) * TILE] * SCALE + btab[h, table])
                top = jnp.maximum(jnp.maximum(terms[0], terms[1]), jnp.maximum(terms[2], terms[3]))
                top = jnp.broadcast_to(jnp.max(top, axis=1, keepdims=True), (TILE, HD))
                if d > 0:
                    old = m_scr[i, rows, :]
                    top = jnp.maximum(old, top)
                    ratio = jnp.exp2(old - top)
                    acc[i, rows, :] = acc[i, rows, :] * jnp.concatenate([ratio, ratio], axis=1)
                m_scr[i, rows, :] = top
                for t in range(4):
                    p_scr[rows, t * TILE:(t + 1) * TILE] = jnp.exp2(terms[t] - top).astype(jnp.bfloat16)
            vx = jnp.concatenate([values[...], jnp.ones((TOK, HD), jnp.bfloat16)], axis=1)
            more = jnp.dot(p_scr[...], vx, preferred_element_type=jnp.float32)
            acc[i] = more if d == 0 else acc[i] + more
            if last:
                for h in range(HEADS):
                    rows = slice(h * TILE, (h + 1) * TILE)
                    out = acc[i, rows, :HD] / acc[i, rows, HD:]
                    att[zl, pl.ds(pl.multiple_of(i * TILE, TILE), TILE), h * HD:(h + 1) * HD] = out.astype(jnp.bfloat16)
                send_att(i).start()
            return carry

        lax.fori_loop(0, TOK // TILE, tile, 0)

    attend(0, k_ref, v_ref)
    kv_arrived(1)
    start(kv_copies(kbuf.at[1], vbuf.at[1], 3, 1, after))

    @pl.when(core == 0)
    def _():
        start(kv_copies(kbuf.at[1], vbuf.at[1], 2, 3, sibling))

    @pl.when(core == 1)
    def _():
        start(kv_copies(kbuf.at[1], vbuf.at[1], 0, 2, sibling))

    ring_begin()
    attend(2, kbuf.at[1], vbuf.at[1])
    kv_arrived(0)
    attend(1, kbuf.at[0], vbuf.at[0])
    ring_step(0)
    kv_arrived(3)

    @pl.when(core == 1)
    def _():
        start(kv_copies(kbuf.at[3], vbuf.at[3], 2, 3, sibling))

    attend(4, kbuf.at[3], vbuf.at[3])
    ring_step(1)
    kv_arrived(2)
    attend(3, kbuf.at[2], vbuf.at[2], last=True)
    ring_step(2)
    ring_step(3)

    for i in range(TOK // TILE):
        rows = att.at[1 - zl, pl.ds(i * TILE, TILE)]
        remote(rows, rows, a_send.at[i], a_recv.at[i], partner).wait_recv()
    for n in range(NY):
        shared(n).wait_recv()

    def far_copy(blk):
        return remote(part.at[blk, :, xo], far.at[blk], far_send.at[blk], far_recv.at[blk], x_up if blk < 2 else x_down)

    def near_copy(way, blk):
        return remote(part.at[blk, :, xr if way == 0 else xl], near.at[way, blk], near_send.at[way, blk],
                      near_recv.at[way, blk], x_up if way == 0 else x_down)

    def zx_copy(blk):
        return remote(zout.at[blk], zin.at[blk], zx_send.at[blk], zx_recv.at[blk], partner)

    def project(blk):
        side, low = blk // 2, (blk % 2) * (NY // 2)
        sums = jnp.zeros((TOK, COLS), jnp.float32)
        for a in range(2):
            rows = wg[a, side, low:low + NY // 2].reshape(COLS, FEAT)
            sums = sums + lax.dot_general(att[a], rows, NT, preferred_element_type=jnp.float32)
        part[blk] = sums.astype(jnp.bfloat16).reshape(2, NX, ROWS, COLS)

    order = (0, 2, 1, 3)
    for blk in order:
        project(blk)
        far_copy(blk).start()
    for blk in order:
        near_copy(1 if blk < 2 else 0, blk).start()
    for blk in order:
        far_copy(blk).wait_recv()
        way = 0 if blk < 2 else 1
        to = xr if way == 0 else xl
        part[blk, :, to] = (part[blk, :, to].astype(jnp.float32) + far[blk].astype(jnp.float32)).astype(jnp.bfloat16)
        near_copy(way, blk).start()
    for blk in order:
        for way in (1, 0) if blk < 2 else (0, 1):
            near_copy(way, blk).wait_recv()

        def whole(b):
            return (part[blk, b, x].astype(jnp.float32) + near[0, blk, b].astype(jnp.float32)
                    + near[1, blk, b].astype(jnp.float32)).astype(jnp.bfloat16)

        zout[blk] = whole(1 - zl)
        zx_copy(blk).start()
        out_ref[:, pl.ds(pl.multiple_of(zl * 4 * COLS + blk * COLS, COLS), COLS)] = whole(zl)
    for blk in order:
        zx_copy(blk).wait_recv()
        out_ref[:, pl.ds(pl.multiple_of((1 - zl) * 4 * COLS + blk * COLS, COLS), COLS)] = zin[blk]

    for c in kv_copies(k_ref, v_ref, 1, 0, after) + kv_copies(k_ref, v_ref, 3, 1, after):
        c.wait_send()
    for n in (2, 3):
        for c in kv_copies(k_ref, v_ref, 0, n, sibling):
            c.wait_send()
    for j in range(1, NZ):
        z_copy(j).wait_send()

    @pl.when(half != zl)
    def _():
        z_copy(0).wait_send()

    for n in range(PLUS):
        ring_up(n).wait_send()
    for n in range(MINUS):
        ring_down(n).wait_send()
    for n in range(NY):
        share(n).wait_send()
    for i in range(TOK // TILE):
        send_att(i).wait_send()
    for blk in order:
        far_copy(blk).wait_send()
        near_copy(0, blk).wait_send()
        near_copy(1, blk).wait_send()
        zx_copy(blk).wait_send()


def on_device(query_feats, key_feats, value_feats, span_class, ramp_width, doc_lengths, out_proj):
    bf16, f32 = jnp.bfloat16, jnp.float32
    dma = pltpu.SemaphoreType.DMA
    vmem = pl.BlockSpec(memory_space=pltpu.VMEM)
    smem = pl.BlockSpec(memory_space=pltpu.SMEM)
    return pl.pallas_call(
        kernel,
        out_shape=jax.ShapeDtypeStruct((ROWS, 8 * COLS), bf16),
        in_specs=[vmem] * 4 + [smem] * 3,
        out_specs=vmem,
        scratch_shapes=[
            pltpu.VMEM((4, TOK, HD), bf16),
            pltpu.VMEM((4, TOK, HD), bf16),
            pltpu.VMEM((4, HEADS * TILE, 2 * HD), bf16),
            pltpu.VMEM((5, TOK, HD), bf16),
            pltpu.VMEM((HEADS, 5, TILE, HD), f32),
            pltpu.VMEM((HEADS * TILE, TOK), f32),
            pltpu.VMEM((HEADS * TILE, TOK), bf16),
            pltpu.VMEM((4, HEADS * TILE, HD), f32),
            pltpu.VMEM((4, HEADS * TILE, 2 * HD), f32),
            pltpu.VMEM((2, TOK, FEAT), bf16),
            pltpu.VMEM((2, 2, NY, 2, ROWS, FEAT), bf16),
            pltpu.VMEM((4, 2, NX, ROWS, COLS), bf16),
            pltpu.VMEM((4, 2, ROWS, COLS), bf16),
            pltpu.VMEM((2, 4, 2, ROWS, COLS), bf16),
            pltpu.VMEM((4, ROWS, COLS), bf16),
            pltpu.VMEM((4, ROWS, COLS), bf16),
            dma((4, 2)), dma((4, 2)), dma((NZ,)), dma((2, 2)),
            dma((PLUS,)), dma((PLUS,)), dma((MINUS,)), dma((MINUS,)),
            dma((NY,)), dma((NY,)), dma((4,)), dma((4,)),
            dma((4,)), dma((4,)), dma((2, 4)), dma((2, 4)),
            dma((4,)), dma((4,)),
        ],
        compiler_params=pltpu.CompilerParams(
            collective_id=0, has_side_effects=True, vmem_limit_bytes=48 * 2**20),
        cost_estimate=pl.CostEstimate(flops=8 * 10**9, bytes_accessed=2 * 10**6, transcendentals=6 * 10**6),
        name="layer",
    )(query_feats, key_feats, value_feats, out_proj, span_class, ramp_width, doc_lengths)


def solution(mesh):
    split = P("seq", "head")
    return jax.shard_map(
        on_device, mesh=mesh, in_specs=(split, split, split, P(), P(), P(), split),
        out_specs=P(("seq", "head"), None), check_vma=False)
```

```python
import math

import jax
import jax.numpy as jnp
from jax import lax
from jax.experimental import pallas as pl
from jax.experimental.pallas import tpu as pltpu
from jax.sharding import PartitionSpec as P

HD = 128
TILE = 128
HEADS = 4
TOK = 512
FEAT = HEADS * HD
NZ, NY, NX = 4, 8, 4
NDOCS = 16
ROWS = 64
UP, DOWN = 2, 4
LOW = -1e30
MESH = pl.DeviceIdType.MESH
NT = (((1,), (1,)), ((), ()))
SCALE = math.log2(math.e) / math.sqrt(HD)


def kernel(q_hbm, k_hbm, v_hbm, w_hbm, span_hbm, ramp_hbm, doc_hbm, out_ref,
           q_ref, k_ref, v_ref, w_ref, span_ref, ramp_ref, doc_ref,
           kbuf, vbuf, qx, kf, btab, s_one, s_two, p_one, p_two, m_scr, acc, att, wg, part,
           far, near, zout, zin,
           khop, vhop, hop_send, hop_recv, in_sem, kv_send, kv_recv, z_send, z_recv, p_send, p_recv, m_send, m_recv,
           s_send, s_recv, a_send, a_recv, far_send, far_recv, near_send, near_recv,
           zx_send, zx_recv):
    loads = [pltpu.make_async_copy(src, dst, in_sem.at[n]) for n, (src, dst) in enumerate((
        (doc_hbm, doc_ref), (span_hbm, span_ref), (ramp_hbm, ramp_ref), (k_hbm, k_ref),
        (v_hbm, v_ref), (w_hbm, w_ref), (q_hbm, q_ref)))]
    for c in loads:
        c.start()
    s_scr, p_scr = (s_one, s_two), (p_one, p_two)
    seq = lax.axis_index("seq")
    head = lax.axis_index("head")
    core = lax.rem(seq, 2)
    y = lax.rem(seq // 2, NY)
    zh = seq // (2 * NY)
    x = lax.rem(head, NX)
    zl = head // NX
    half = zh // 2
    n_seq = 2 * NY * NZ
    chip = seq // 2
    last_chip = NY * NZ - 1
    leaves = zh < NZ - 1
    came = zh > 0

    def at(zh_, y_, c_, zl_, x_):
        return ((zh_ * NY + y_) * 2 + c_, zl_ * NX + x_)

    after = (lax.rem(seq + 2, n_seq), head)
    before = (lax.rem(seq + n_seq - 2, n_seq), head)
    sibling = at(zh, y, 1 - core, zl, x)
    y_up = at(zh, lax.rem(y + 1, NY), core, zl, x)
    y_down = at(zh, lax.rem(y + NY - 1, NY), core, zl, x)
    xr, xl = lax.rem(x + 1, NX), lax.rem(x + NX - 1, NX)
    xo = lax.rem(x + 2, NX)
    x_up = at(zh, y, core, zl, xr)
    x_down = at(zh, y, core, zl, xl)
    z_next = at(lax.rem(zh + 1, NZ), y, core, zl, x)
    partner = at(zh, y, core, 1 - zl, x)

    @pl.when(chip < 2)
    def _():
        kbuf[...] = jnp.zeros_like(kbuf)
        vbuf[...] = jnp.zeros_like(vbuf)

    barrier = pltpu.get_barrier_semaphore()
    greet = [sibling, y_up, y_down, x_up, x_down, partner]
    for j in range(1, NZ):
        for b in range(2):
            greet.append(at(lax.rem(zh + j, NZ), y, core, b, x))
    for device in greet:
        pl.semaphore_signal(barrier, inc=1, device_id=device, device_id_type=MESH)

    @pl.when(chip < last_chip)
    def _():
        pl.semaphore_signal(barrier, inc=1, device_id=after, device_id_type=MESH)

    @pl.when(chip > 0)
    def _():
        pl.semaphore_signal(barrier, inc=1, device_id=before, device_id_type=MESH)

    for c in loads:
        c.wait()

    pl.semaphore_wait(barrier, len(greet) + jnp.where(chip < last_chip, 1, 0) + jnp.where(chip > 0, 1, 0))

    def remote(src, dst, send, recv, device):
        return pltpu.make_async_remote_copy(
            src_ref=src, dst_ref=dst, send_sem=send, recv_sem=recv,
            device_id=device, device_id_type=MESH)

    def kv_copies(k_src, v_src, slot, n, device):
        return (remote(k_src, kbuf.at[slot], kv_send.at[n, 0], kv_recv.at[slot, 0], device),
                remote(v_src, vbuf.at[slot], kv_send.at[n, 1], kv_recv.at[slot, 1], device))

    def start(copies):
        for c in copies:
            c.start()

    def start_if(condition, copies):
        @pl.when(condition)
        def _():
            start(copies)

    def sent_if(condition, copies):
        @pl.when(condition)
        def _():
            for c in copies:
                c.wait_send()

    def kv_arrived(slot, condition):
        @pl.when(condition)
        def _():
            for c in kv_copies(k_ref, v_ref, slot, 0, sibling):
                c.wait_recv()

    k_on, v_on = kv_copies(k_ref, v_ref, 1, 0, after)
    k_aside = remote(kbuf.at[1], khop, hop_send.at[1], hop_recv.at[1], z_next)
    v_aside = remote(v_ref, vhop, hop_send.at[0], hop_recv.at[0], z_next)
    k_second, v_second = kv_copies(kbuf.at[1], vbuf.at[1], 3, 1, after)
    sends = dict(
        k_on=(chip < last_chip, (k_on,)),
        v_on=(y < NY - 1, (v_on,)),
        v_aside=((y == NY - 1) & leaves, (v_aside,)),
        v_after=((y == NY - 1) & came, kv_copies(khop, vhop, 1, 4, y_up)[1:]),
        v_second=((chip > 0) & (chip < last_chip), (v_second,)),
        k_second=((chip > 0) & (y < NY - 1), (k_second,)),
        k_aside=((y == NY - 1) & leaves, (k_aside,)),
        k_after=((y == NY - 1) & came, kv_copies(khop, vhop, 3, 4, y_up)[:1]),
        own_over=(core == 0, kv_copies(k_ref, v_ref, 0, 2, sibling)),
        first_over=((core == 1) & (chip > 0), kv_copies(kbuf.at[1], vbuf.at[1], 0, 2, sibling)),
        even_over=((core == 0) & (chip > 0), kv_copies(kbuf.at[1], vbuf.at[1], 2, 3, sibling)),
        odd_over=((core == 1) & (chip > 1), kv_copies(kbuf.at[3], vbuf.at[3], 2, 3, sibling)),
    )
    for name in ("k_on", "v_aside", "v_on", "own_over"):
        start_if(*sends[name])

    mine = (zl, lax.rem(zh, 2))

    def z_copy(j):
        target = at(lax.rem(zh + j, NZ), y, core, half, x)
        return remote(w_ref, wg.at[mine[0], mine[1], y, core], z_send.at[j], z_recv.at[mine[0], mine[1]], target)

    for j in range(1, NZ):
        z_copy(j).start()

    @pl.when(half == zl)
    def _():
        pltpu.make_async_copy(w_ref, wg.at[mine[0], mine[1], y, core], z_recv.at[mine[0], mine[1]]).start()

    @pl.when(half != zl)
    def _():
        z_copy(0).start()

    def chunk(n, j, c_):
        return wg.at[:, j, lax.rem(y + n, NY), c_]

    def ring_up(n, j):
        src = chunk(NY - n, j, core)
        return remote(src, src, p_send.at[n, j], p_recv.at[n, j], y_up)

    def ring_down(n, j):
        src = chunk(n, j, core)
        return remote(src, src, m_send.at[n, j], m_recv.at[n, j], y_down)

    def got_up(n, j):
        src = chunk(NY - n - 1, j, core)
        return remote(src, src, p_send.at[n, j], p_recv.at[n, j], y_up)

    def got_down(n, j):
        src = chunk(n + 1, j, core)
        return remote(src, src, m_send.at[n, j], m_recv.at[n, j], y_down)

    def share(n, j):
        src = chunk(n, j, core)
        return remote(src, src, s_send.at[n, j], s_recv.at[n, j], sibling)

    def shared(n, j):
        src = chunk(n, j, 1 - core)
        return remote(src, src, s_send.at[n, j], s_recv.at[n, j], sibling)

    def ring_begin():
        for j in range(2):
            for a in range(2):
                remote(w_ref, wg.at[a, j, y, core], z_send.at[0], z_recv.at[a, j], sibling).wait_recv()
            ring_down(0, j).start()
            ring_up(0, j).start()
            share(0, j).start()

    def ring_step(n, j):
        def down():
            got_down(n, j).wait_recv()
            if n + 1 < DOWN:
                ring_down(n + 1, j).start()
            elif n + 1 == DOWN:
                @pl.when(j == 0)
                def _():
                    ring_down(n + 1, j).start()

            share(n + 1, j).start()

        def up():
            got_up(n, j).wait_recv()
            if n + 1 < UP:
                ring_up(n + 1, j).start()
            elif n + 1 == UP:
                @pl.when(j == 1)
                def _():
                    ring_up(n + 1, j).start()

            share(NY - n - 1, j).start()

        down()
        if n < UP:
            up()
        elif n == UP:
            pl.when(j == 1)(up)

    def ring_end():
        got_down(DOWN, 0).wait_recv()
        share(DOWN + 1, 0).start()

    lane = lax.broadcasted_iota(jnp.int32, (1, HD), 1)
    starts = jnp.zeros((1, HD), jnp.int32)
    ends = jnp.zeros((1, HD), jnp.int32)
    total = jnp.int32(0)
    for n in range(NDOCS):
        starts = jnp.where(lane == n, total, starts)
        total = total + doc_ref[n]
        ends = jnp.where(lane == n, total, ends)
    row_of = lax.broadcasted_iota(jnp.int32, (TILE, HD), 0)
    lane_of = lax.broadcasted_iota(jnp.int32, (TILE, HD), 1)
    named = lane_of < NDOCS

    def features(n, carry):
        pos = seq * TOK + n * TILE + row_of
        inside = (pos >= starts) & (pos < ends)
        other = jnp.where(named & jnp.logical_not(inside), 1.0, 0.0).astype(jnp.bfloat16)
        for h in range(HEADS):
            qx[n, h * TILE:(h + 1) * TILE, HD:] = other
            qx[n, h * TILE:(h + 1) * TILE, :HD] = q_ref[pl.ds(pl.multiple_of(n * TILE, TILE), TILE), h * HD:(h + 1) * HD]
        for d in range(5):
            key_pos = pos - d * TOK
            hidden = ((key_pos >= starts) & (key_pos < ends)) | (key_pos < 0)
            kf[d, pl.ds(pl.multiple_of(n * TILE, TILE), TILE), :] = jnp.where(named & hidden, LOW, 0.0).astype(jnp.bfloat16)
        return carry

    lax.fori_loop(0, TOK // TILE, features, 0)

    diff = (row_of - lane_of).astype(jnp.float32)

    def weight(distance_left, ramp, seen):
        w = jnp.clip(distance_left / ramp, 0.0, 1.0)
        keep = (w > 0.0) & seen
        return jnp.where(keep, jnp.log2(jnp.where(keep, w, 1.0)), LOW)

    for h in range(HEADS):
        ramp = ramp_ref[head * HEADS + h].astype(jnp.float32)
        span = span_ref[head * HEADS + h].astype(jnp.float32) * float(TILE)
        always = diff < 1000.0
        btab[h, 0] = jnp.zeros((TILE, HD), jnp.float32)
        btab[h, 1] = weight(float(TILE) - diff, ramp, always)
        btab[h, 2] = weight(-diff, ramp, always)
        btab[h, 3] = weight(span - diff, ramp, diff >= 0.0)
        btab[h, 4] = jnp.full((TILE, HD), LOW, jnp.float32)

    def send_att(i):
        rows = att.at[zl, pl.ds(pl.multiple_of(i * TILE, TILE), TILE)]
        return remote(rows, rows, a_send.at[i], a_recv.at[i], partner)

    def attend(pair, d, keys, values):
        for one in range(2):
            kx = jnp.concatenate([keys[...], kf[d]], axis=1)
            s_scr[one][...] = lax.dot_general(qx[2 * pair + one], kx, NT, preferred_element_type=jnp.float32)
        for one in range(2):
            i = 2 * pair + one
            for h in range(HEADS):
                span = span_ref[head * HEADS + h]
                rows = slice(h * TILE, (h + 1) * TILE)
                terms = []
                for t in range(4):
                    delta = 4 * d + i - t
                    over = delta - span
                    table = jnp.where(over > 0, 4, jnp.maximum(over + 2, 0))
                    table = jnp.where(delta > 0, table, jnp.where(delta == 0, 3, 4))
                    terms.append(s_scr[one][rows, t * TILE:(t + 1) * TILE] * SCALE + btab[h, table])
                top = jnp.maximum(jnp.maximum(terms[0], terms[1]), jnp.maximum(terms[2], terms[3]))
                top = jnp.broadcast_to(jnp.max(top, axis=1, keepdims=True), (TILE, HD))
                if d > 0:
                    old = m_scr[i, rows, :]
                    top = jnp.maximum(old, top)
                    ratio = jnp.exp2(old - top)
                    acc[i, rows, :] = acc[i, rows, :] * jnp.concatenate([ratio, ratio], axis=1)
                m_scr[i, rows, :] = top
                for t in range(4):
                    p_scr[one][rows, t * TILE:(t + 1) * TILE] = jnp.exp2(terms[t] - top).astype(jnp.bfloat16)
            vx = jnp.concatenate([values[...], jnp.ones((TOK, HD), jnp.bfloat16)], axis=1)
            more = jnp.dot(p_scr[one][...], vx, preferred_element_type=jnp.float32)
            acc[i] = more if d == 0 else acc[i] + more

    def over_pairs(body):
        def step(pair, carry):
            body(pair)
            return carry

        lax.fori_loop(0, 2, step, 0)

    @over_pairs
    def _(pair):
        attend(pair, 0, k_ref, v_ref)

    @pl.when((y == NY - 1) & came)
    def _():
        v_aside.wait_recv()

    start_if(*sends["v_after"])
    ring_begin()
    kv_arrived(1, chip > 0)
    for name in ("k_second", "k_aside", "v_second", "even_over", "first_over"):
        start_if(*sends[name])

    @over_pairs
    def _(pair):
        attend(pair, 2, kbuf.at[1], vbuf.at[1])
        ring_step(0, pair)

    @pl.when((y == NY - 1) & came)
    def _():
        k_aside.wait_recv()

    start_if(*sends["k_after"])
    kv_arrived(0, (core == 1) | (chip > 0))

    @over_pairs
    def _(pair):
        attend(pair, 1, kbuf.at[0], vbuf.at[0])
        ring_step(1, pair)

    late = (y < 2) & came

    @pl.when(late)
    def _():
        ring_step(2, 0)
        ring_step(2, 1)

    kv_arrived(3, chip > 1)
    start_if(*sends["odd_over"])
    kv_arrived(2, (chip > 1) | ((core == 1) & (chip > 0)))

    @over_pairs
    def _(pair):
        attend(pair, 4, kbuf.at[3], vbuf.at[3])
        attend(pair, 3, kbuf.at[2], vbuf.at[2])
        for one in range(2):
            i = 2 * pair + one
            for h in range(HEADS):
                rows = slice(h * TILE, (h + 1) * TILE)
                out = acc[i, rows, :HD] / acc[i, rows, HD:]
                att[zl, pl.ds(pl.multiple_of(i * TILE, TILE), TILE), h * HD:(h + 1) * HD] = out.astype(jnp.bfloat16)
            send_att(i).start()

        @pl.when(jnp.logical_not(late))
        def _():
            ring_step(2, pair)

    for i in range(TOK // TILE):
        rows = att.at[1 - zl, pl.ds(i * TILE, TILE)]
        remote(rows, rows, a_send.at[i], a_recv.at[i], partner).wait_recv()

    pairs = ((0, 1), (7, 2), (6, 3), (4, 5))

    def far_copy(g, j):
        return remote(part.at[g, j, :, xo], far.at[g, j], far_send.at[g, j], far_recv.at[g, j], (x_up, x_down)[j])

    def near_copy(way, g, j):
        return remote(part.at[g, j, :, (xr, xl)[way]], near.at[way, g, j], near_send.at[way, g, j],
                      near_recv.at[way, g, j], (x_up, x_down)[way])

    def zx_copy(g):
        return remote(zout.at[g], zin.at[g], zx_send.at[g], zx_recv.at[g], partner)

    def project(g):
        for p, n in enumerate(pairs[g]):
            for j in range(2):
                shared(n, j).wait_recv()
            place = lax.rem(y + n, NY)
            sums = None
            for a in range(2):
                rows = wg[a, :, place].reshape(4 * ROWS, FEAT)
                more = lax.dot_general(att[a], rows, NT, preferred_element_type=jnp.float32)
                sums = more if sums is None else sums + more
            for j in range(2):
                part[g, j, :, :, :, p * TILE:(p + 1) * TILE] = sums[:, j * TILE:(j + 1) * TILE].astype(
                    jnp.bfloat16).reshape(2, NX, ROWS, TILE)
        for j in range(2):
            far_copy(g, j).start()
        for j in range(2):
            near_copy(1 - j, g, j).start()

    def pass_on(g):
        for j in range(2):
            far_copy(g, j).wait_recv()
            to = (xr, xl)[j]
            part[g, j, :, to] = (part[g, j, :, to].astype(jnp.float32) + far[g, j].astype(jnp.float32)).astype(jnp.bfloat16)
            near_copy(j, g, j).start()

    def columns(side, g, j, p):
        return pl.ds(pl.multiple_of(((side * 2 + j) * NY + lax.rem(y + pairs[g][p], NY)) * TILE, TILE), TILE)

    def finish(g):
        for j in range(2):
            for way in (1 - j, j):
                near_copy(way, g, j).wait_recv()

            def whole(b):
                return (part[g, j, b, x].astype(jnp.float32) + near[0, g, j, b].astype(jnp.float32)
                        + near[1, g, j, b].astype(jnp.float32)).astype(jnp.bfloat16)

            zout[g, j] = whole(1 - zl)
            kept = whole(zl)
            for p in range(2):
                out_ref[:, columns(zl, g, j, p)] = kept[:, p * TILE:(p + 1) * TILE]
        zx_copy(g).start()

    def place(g):
        zx_copy(g).wait_recv()
        for j in range(2):
            for p in range(2):
                out_ref[:, columns(1 - zl, g, j, p)] = zin[g, j, :, p * TILE:(p + 1) * TILE]

    project(0)
    ring_step(3, 0)
    project(1)
    pass_on(0)
    ring_step(3, 1)
    project(2)
    pass_on(1)
    ring_end()
    project(3)
    finish(0)
    pass_on(2)
    finish(1)
    pass_on(3)
    finish(2)
    place(0)
    place(1)
    finish(3)
    place(2)
    place(3)

    for condition, copies in sends.values():
        sent_if(condition, copies)
    for j in range(1, NZ):
        z_copy(j).wait_send()

    @pl.when(half != zl)
    def _():
        z_copy(0).wait_send()

    for j in range(2):
        for n in range(UP + j):
            ring_up(n, j).wait_send()
        for n in range(DOWN + 1 - j):
            ring_down(n, j).wait_send()
        for n in range(NY):
            share(n, j).wait_send()
    for i in range(TOK // TILE):
        send_att(i).wait_send()
    for g in range(4):
        for j in range(2):
            far_copy(g, j).wait_send()
            near_copy(0, g, j).wait_send()
            near_copy(1, g, j).wait_send()
        zx_copy(g).wait_send()


def on_device(query_feats, key_feats, value_feats, span_class, ramp_width, doc_lengths, out_proj):
    bf16, f32 = jnp.bfloat16, jnp.float32
    dma = pltpu.SemaphoreType.DMA
    return pl.pallas_call(
        kernel,
        out_shape=jax.ShapeDtypeStruct((ROWS, 8 * FEAT), bf16),
        in_specs=[pl.BlockSpec(memory_space=pltpu.HBM)] * 7,
        out_specs=pl.BlockSpec(memory_space=pltpu.VMEM),
        scratch_shapes=[
            pltpu.VMEM((TOK, FEAT), bf16),
            pltpu.VMEM((TOK, HD), bf16),
            pltpu.VMEM((TOK, HD), bf16),
            pltpu.VMEM((ROWS, FEAT), bf16),
            pltpu.SMEM((32,), jnp.int32),
            pltpu.SMEM((32,), jnp.int32),
            pltpu.SMEM((NDOCS,), jnp.int32),
            pltpu.VMEM((4, TOK, HD), bf16),
            pltpu.VMEM((4, TOK, HD), bf16),
            pltpu.VMEM((4, HEADS * TILE, 2 * HD), bf16),
            pltpu.VMEM((5, TOK, HD), bf16),
            pltpu.VMEM((HEADS, 5, TILE, HD), f32),
            pltpu.VMEM((HEADS * TILE, TOK), f32),
            pltpu.VMEM((HEADS * TILE, TOK), f32),
            pltpu.VMEM((HEADS * TILE, TOK), bf16),
            pltpu.VMEM((HEADS * TILE, TOK), bf16),
            pltpu.VMEM((4, HEADS * TILE, HD), f32),
            pltpu.VMEM((4, HEADS * TILE, 2 * HD), f32),
            pltpu.VMEM((2, TOK, FEAT), bf16),
            pltpu.VMEM((2, 2, NY, 2, ROWS, FEAT), bf16),
            pltpu.VMEM((4, 2, 2, NX, ROWS, 2 * TILE), bf16),
            pltpu.VMEM((4, 2, 2, ROWS, 2 * TILE), bf16),
            pltpu.VMEM((2, 4, 2, 2, ROWS, 2 * TILE), bf16),
            pltpu.VMEM((4, 2, ROWS, 2 * TILE), bf16),
            pltpu.VMEM((4, 2, ROWS, 2 * TILE), bf16),
            pltpu.VMEM((TOK, HD), bf16), pltpu.VMEM((TOK, HD), bf16), dma((2,)), dma((2,)), dma((7,)), dma((5, 2)), dma((4, 2)), dma((NZ,)), dma((2, 2)),
            dma((UP + 1, 2)), dma((UP + 1, 2)), dma((DOWN + 1, 2)), dma((DOWN + 1, 2)),
            dma((NY, 2)), dma((NY, 2)), dma((4,)), dma((4,)),
            dma((4, 2)), dma((4, 2)), dma((2, 4, 2)), dma((2, 4, 2)),
            dma((4,)), dma((4,)),
        ],
        compiler_params=pltpu.CompilerParams(
            collective_id=0, has_side_effects=True, vmem_limit_bytes=60 * 2**20),
        cost_estimate=pl.CostEstimate(flops=8 * 10**9, bytes_accessed=2 * 10**6, transcendentals=6 * 10**6),
        name="layer",
    )(query_feats, key_feats, value_feats, out_proj, span_class, ramp_width, doc_lengths)


def solution(mesh):
    split = P("seq", "head")
    return jax.shard_map(
        on_device, mesh=mesh, in_specs=(split, split, split, P(), P(), P(), split),
        out_specs=P(("seq", "head"), None), check_vma=False)
```

```python
import math

import jax
import jax.numpy as jnp
from jax import lax
from jax.experimental import pallas as pl
from jax.experimental.pallas import tpu as pltpu
from jax.sharding import PartitionSpec as P

HD = 128
TILE = 128
HEADS = 4
TOK = 512
FEAT = HEADS * HD
NZ, NY, NX = 4, 8, 4
NDOCS = 16
ROWS = 64
UP, DOWN = 2, 4
LOW = -1e30
MESH = pl.DeviceIdType.MESH
NT = (((1,), (1,)), ((), ()))
SCALE = math.log2(math.e) / math.sqrt(HD)


def kernel(q_hbm, k_hbm, v_hbm, w_hbm, span_hbm, ramp_hbm, doc_hbm, out_ref,
           q_ref, k_ref, v_ref, w_ref, span_ref, ramp_ref, doc_ref,
           kbuf, vbuf, qx, kf, btab, s_one, s_two, p_one, p_two, m_scr, acc, att, wg, part,
           far, near, zout, zin,
           khop, vhop, hop_send, hop_recv, in_sem, kv_send, kv_recv, z_send, z_recv, p_send, p_recv, m_send, m_recv,
           s_send, s_recv, a_send, a_recv, far_send, far_recv, near_send, near_recv,
           zx_send, zx_recv):
    loads = [pltpu.make_async_copy(src, dst, in_sem.at[n]) for n, (src, dst) in enumerate((
        (doc_hbm, doc_ref), (span_hbm, span_ref), (ramp_hbm, ramp_ref), (k_hbm, k_ref),
        (v_hbm, v_ref), (w_hbm, w_ref), (q_hbm, q_ref)))]
    for c in loads:
        c.start()
    s_scr, p_scr = (s_one, s_two), (p_one, p_two)
    seq = lax.axis_index("seq")
    head = lax.axis_index("head")
    core = lax.rem(seq, 2)
    y = lax.rem(seq // 2, NY)
    zh = seq // (2 * NY)
    x = lax.rem(head, NX)
    zl = head // NX
    half = zh // 2
    n_seq = 2 * NY * NZ
    chip = seq // 2
    last_chip = NY * NZ - 1
    leaves = zh < NZ - 1
    came = zh > 0

    def at(zh_, y_, c_, zl_, x_):
        return ((zh_ * NY + y_) * 2 + c_, zl_ * NX + x_)

    after = (lax.rem(seq + 2, n_seq), head)
    before = (lax.rem(seq + n_seq - 2, n_seq), head)
    sibling = at(zh, y, 1 - core, zl, x)
    y_up = at(zh, lax.rem(y + 1, NY), core, zl, x)
    y_down = at(zh, lax.rem(y + NY - 1, NY), core, zl, x)
    xr, xl = lax.rem(x + 1, NX), lax.rem(x + NX - 1, NX)
    xo = lax.rem(x + 2, NX)
    x_up = at(zh, y, core, zl, xr)
    x_down = at(zh, y, core, zl, xl)
    z_next = at(lax.rem(zh + 1, NZ), y, core, zl, x)
    partner = at(zh, y, core, 1 - zl, x)

    @pl.when(chip < 2)
    def _():
        kbuf[...] = jnp.zeros_like(kbuf)
        vbuf[...] = jnp.zeros_like(vbuf)

    barrier = pltpu.get_barrier_semaphore()
    greet = [sibling, y_up, y_down, x_up, x_down, partner]
    for j in range(1, NZ):
        for b in range(2):
            greet.append(at(lax.rem(zh + j, NZ), y, core, b, x))
    for device in greet:
        pl.semaphore_signal(barrier, inc=1, device_id=device, device_id_type=MESH)

    @pl.when(chip < last_chip)
    def _():
        pl.semaphore_signal(barrier, inc=1, device_id=after, device_id_type=MESH)

    @pl.when(chip > 0)
    def _():
        pl.semaphore_signal(barrier, inc=1, device_id=before, device_id_type=MESH)

    for c in loads:
        c.wait()

    pl.semaphore_wait(barrier, len(greet) + jnp.where(chip < last_chip, 1, 0) + jnp.where(chip > 0, 1, 0))

    def remote(src, dst, send, recv, device):
        return pltpu.make_async_remote_copy(
            src_ref=src, dst_ref=dst, send_sem=send, recv_sem=recv,
            device_id=device, device_id_type=MESH)

    def kv_copies(k_src, v_src, slot, n, device):
        return (remote(k_src, kbuf.at[slot], kv_send.at[n, 0], kv_recv.at[slot, 0], device),
                remote(v_src, vbuf.at[slot], kv_send.at[n, 1], kv_recv.at[slot, 1], device))

    def start(copies):
        for c in copies:
            c.start()

    def start_if(condition, copies):
        @pl.when(condition)
        def _():
            start(copies)

    def sent_if(condition, copies):
        @pl.when(condition)
        def _():
            for c in copies:
                c.wait_send()

    def kv_arrived(slot, condition):
        @pl.when(condition)
        def _():
            for c in kv_copies(k_ref, v_ref, slot, 0, sibling):
                c.wait_recv()

    k_on, v_on = kv_copies(k_ref, v_ref, 1, 0, after)
    k_aside = remote(kbuf.at[1], khop, hop_send.at[1], hop_recv.at[1], z_next)
    v_aside = remote(v_ref, vhop, hop_send.at[0], hop_recv.at[0], z_next)
    k_second, v_second = kv_copies(kbuf.at[1], vbuf.at[1], 3, 1, after)
    sends = dict(
        k_on=(chip < last_chip, (k_on,)),
        v_on=(y < NY - 1, (v_on,)),
        v_aside=((y == NY - 1) & leaves, (v_aside,)),
        v_after=((y == NY - 1) & came, kv_copies(khop, vhop, 1, 4, y_up)[1:]),
        v_second=((chip > 0) & (chip < last_chip), (v_second,)),
        k_second=((chip > 0) & (y < NY - 1), (k_second,)),
        k_aside=((y == NY - 1) & leaves, (k_aside,)),
        k_after=((y == NY - 1) & came, kv_copies(khop, vhop, 3, 4, y_up)[:1]),
        own_over=(core == 0, kv_copies(k_ref, v_ref, 0, 2, sibling)),
        first_over=((core == 1) & (chip > 0), kv_copies(kbuf.at[1], vbuf.at[1], 0, 2, sibling)),
        even_over=((core == 0) & (chip > 0), kv_copies(kbuf.at[1], vbuf.at[1], 2, 3, sibling)),
        odd_over=((core == 1) & (chip > 1), kv_copies(kbuf.at[3], vbuf.at[3], 2, 3, sibling)),
    )
    for name in ("k_on", "v_aside", "v_on", "own_over"):
        start_if(*sends[name])

    mine = (zl, lax.rem(zh, 2))

    def part_of(ref, r):
        return ref.at[pl.ds(r * (ROWS // 2), ROWS // 2)]

    def z_copy(j, r):
        target = at(lax.rem(zh + j, NZ), y, core, half, x)
        return remote(part_of(w_ref, r), part_of(wg.at[mine[0], mine[1], y, core], r), z_send.at[j, r],
                      z_recv.at[mine[0], mine[1], r], target)

    for r in range(2):
        for j in range(1, NZ):
            z_copy(j, r).start()

        @pl.when(half == zl)
        def _():
            pltpu.make_async_copy(part_of(w_ref, r), part_of(wg.at[mine[0], mine[1], y, core], r),
                                  z_recv.at[mine[0], mine[1], r]).start()

        @pl.when(half != zl)
        def _():
            z_copy(0, r).start()

    def chunk(n, j, c_):
        rows = pl.ds(pl.multiple_of(j * (ROWS // 2), ROWS // 2), ROWS // 2)
        return wg.at[:, :, lax.rem(y + n, NY), c_, rows]

    def ring_up(n, j):
        src = chunk(NY - n, j, core)
        return remote(src, src, p_send.at[n, j], p_recv.at[n, j], y_up)

    def ring_down(n, j):
        src = chunk(n, j, core)
        return remote(src, src, m_send.at[n, j], m_recv.at[n, j], y_down)

    def got_up(n, j):
        src = chunk(NY - n - 1, j, core)
        return remote(src, src, p_send.at[n, j], p_recv.at[n, j], y_up)

    def got_down(n, j):
        src = chunk(n + 1, j, core)
        return remote(src, src, m_send.at[n, j], m_recv.at[n, j], y_down)

    def share(n, j):
        src = chunk(n, j, core)
        return remote(src, src, s_send.at[n, j], s_recv.at[n, j], sibling)

    def shared(n, j):
        src = chunk(n, j, 1 - core)
        return remote(src, src, s_send.at[n, j], s_recv.at[n, j], sibling)

    def ring_begin():
        for j in range(2):
            for a in range(2):
                for b in range(2):
                    remote(part_of(w_ref, j), part_of(wg.at[a, b, y, core], j), z_send.at[0, j],
                           z_recv.at[a, b, j], sibling).wait_recv()
            ring_down(0, j).start()
            ring_up(0, j).start()
            share(0, j).start()

    def ring_step(n, j):
        def down():
            got_down(n, j).wait_recv()
            if n + 1 < DOWN:
                ring_down(n + 1, j).start()
            elif n + 1 == DOWN:
                @pl.when(j == 0)
                def _():
                    ring_down(n + 1, j).start()

            share(n + 1, j).start()

        def up():
            got_up(n, j).wait_recv()
            if n + 1 < UP:
                ring_up(n + 1, j).start()
            elif n + 1 == UP:
                @pl.when(j == 1)
                def _():
                    ring_up(n + 1, j).start()

            share(NY - n - 1, j).start()

        down()
        if n < UP:
            up()
        elif n == UP:
            pl.when(j == 1)(up)

    def ring_end():
        got_down(DOWN, 0).wait_recv()
        share(DOWN + 1, 0).start()

    lane = lax.broadcasted_iota(jnp.int32, (1, HD), 1)
    starts = jnp.zeros((1, HD), jnp.int32)
    ends = jnp.zeros((1, HD), jnp.int32)
    total = jnp.int32(0)
    for n in range(NDOCS):
        starts = jnp.where(lane == n, total, starts)
        total = total + doc_ref[n]
        ends = jnp.where(lane == n, total, ends)
    row_of = lax.broadcasted_iota(jnp.int32, (TILE, HD), 0)
    lane_of = lax.broadcasted_iota(jnp.int32, (TILE, HD), 1)
    named = lane_of < NDOCS

    def features(n, carry):
        pos = seq * TOK + n * TILE + row_of
        inside = (pos >= starts) & (pos < ends)
        other = jnp.where(named & jnp.logical_not(inside), 1.0, 0.0).astype(jnp.bfloat16)
        for h in range(HEADS):
            qx[n, h * TILE:(h + 1) * TILE, HD:] = other
            qx[n, h * TILE:(h + 1) * TILE, :HD] = q_ref[pl.ds(pl.multiple_of(n * TILE, TILE), TILE), h * HD:(h + 1) * HD]
        for d in range(5):
            key_pos = pos - d * TOK
            hidden = ((key_pos >= starts) & (key_pos < ends)) | (key_pos < 0)
            kf[d, pl.ds(pl.multiple_of(n * TILE, TILE), TILE), :] = jnp.where(named & hidden, LOW, 0.0).astype(jnp.bfloat16)
        return carry

    lax.fori_loop(0, TOK // TILE, features, 0)

    diff = (row_of - lane_of).astype(jnp.float32)

    def weight(distance_left, ramp, seen):
        w = jnp.clip(distance_left / ramp, 0.0, 1.0)
        keep = (w > 0.0) & seen
        return jnp.where(keep, jnp.log2(jnp.where(keep, w, 1.0)), LOW)

    for h in range(HEADS):
        ramp = ramp_ref[head * HEADS + h].astype(jnp.float32)
        span = span_ref[head * HEADS + h].astype(jnp.float32) * float(TILE)
        always = diff < 1000.0
        btab[h, 0] = jnp.zeros((TILE, HD), jnp.float32)
        btab[h, 1] = weight(float(TILE) - diff, ramp, always)
        btab[h, 2] = weight(-diff, ramp, always)
        btab[h, 3] = weight(span - diff, ramp, diff >= 0.0)
        btab[h, 4] = jnp.full((TILE, HD), LOW, jnp.float32)

    def send_att(i):
        rows = att.at[zl, pl.ds(pl.multiple_of(i * TILE, TILE), TILE)]
        return remote(rows, rows, a_send.at[i], a_recv.at[i], partner)

    def attend(pair, d, keys, values):
        for one in range(2):
            kx = jnp.concatenate([keys[...], kf[d]], axis=1)
            s_scr[one][...] = lax.dot_general(qx[2 * pair + one], kx, NT, preferred_element_type=jnp.float32)
        for one in range(2):
            i = 2 * pair + one
            for h in range(HEADS):
                span = span_ref[head * HEADS + h]
                rows = slice(h * TILE, (h + 1) * TILE)
                terms = []
                for t in range(4):
                    delta = 4 * d + i - t
                    over = delta - span
                    table = jnp.where(over > 0, 4, jnp.maximum(over + 2, 0))
                    table = jnp.where(delta > 0, table, jnp.where(delta == 0, 3, 4))
                    terms.append(s_scr[one][rows, t * TILE:(t + 1) * TILE] * SCALE + btab[h, table])
                top = jnp.maximum(jnp.maximum(terms[0], terms[1]), jnp.maximum(terms[2], terms[3]))
                top = jnp.broadcast_to(jnp.max(top, axis=1, keepdims=True), (TILE, HD))
                if d > 0:
                    old = m_scr[i, rows, :]
                    top = jnp.maximum(old, top)
                    ratio = jnp.exp2(old - top)
                    acc[i, rows, :] = acc[i, rows, :] * jnp.concatenate([ratio, ratio], axis=1)
                m_scr[i, rows, :] = top
                for t in range(4):
                    p_scr[one][rows, t * TILE:(t + 1) * TILE] = jnp.exp2(terms[t] - top).astype(jnp.bfloat16)
            vx = jnp.concatenate([values[...], jnp.ones((TOK, HD), jnp.bfloat16)], axis=1)
            more = jnp.dot(p_scr[one][...], vx, preferred_element_type=jnp.float32)
            acc[i] = more if d == 0 else acc[i] + more

    def over_pairs(body):
        def step(pair, carry):
            body(pair)
            return carry

        lax.fori_loop(0, 2, step, 0)

    @over_pairs
    def _(pair):
        attend(pair, 0, k_ref, v_ref)

    @pl.when((y == NY - 1) & came)
    def _():
        v_aside.wait_recv()

    start_if(*sends["v_after"])
    late = (y == 0) & came

    def relay(now):
        kv_arrived(1, now & (chip > 0))
        for name in ("k_aside", "v_second", "k_second", "even_over", "first_over"):
            start_if(now & sends[name][0], sends[name][1])

    relay(jnp.logical_not(late))
    ring_begin()
    relay(late)

    @over_pairs
    def _(pair):
        attend(pair, 2, kbuf.at[1], vbuf.at[1])

        @pl.when((pair == 1) & (y == NY - 1) & came)
        def _():
            k_aside.wait_recv()
            sends["k_after"][1][0].start()

        ring_step(0, pair)

    kv_arrived(0, (core == 1) | (chip > 0))

    @over_pairs
    def _(pair):
        attend(pair, 1, kbuf.at[0], vbuf.at[0])

    ring_step(1, 0)
    kv_arrived(3, chip > 1)
    start_if(*sends["odd_over"])
    kv_arrived(2, (chip > 1) | ((core == 1) & (chip > 0)))

    @over_pairs
    def _(pair):
        attend(pair, 4, kbuf.at[3], vbuf.at[3])
        attend(pair, 3, kbuf.at[2], vbuf.at[2])
        for one in range(2):
            i = 2 * pair + one
            for h in range(HEADS):
                rows = slice(h * TILE, (h + 1) * TILE)
                out = acc[i, rows, :HD] / acc[i, rows, HD:]
                att[zl, pl.ds(pl.multiple_of(i * TILE, TILE), TILE), h * HD:(h + 1) * HD] = out.astype(jnp.bfloat16)
            send_att(i).start()

        @pl.when(pair == 0)
        def _():
            ring_step(1, 1)

    ring_step(2, 0)
    ring_step(2, 1)
    ring_step(3, 0)

    for i in range(TOK // TILE):
        rows = att.at[1 - zl, pl.ds(i * TILE, TILE)]
        remote(rows, rows, a_send.at[i], a_recv.at[i], partner).wait_recv()

    pairs = ((0, 1), (7, 2), (6, 3), (4, 5))

    def far_copy(g, j):
        return remote(part.at[g, j, :, xo], far.at[g, j], far_send.at[g, j], far_recv.at[g, j], (x_up, x_down)[j])

    def near_copy(way, g, j):
        return remote(part.at[g, j, :, (xr, xl)[way]], near.at[way, g, j], near_send.at[way, g, j],
                      near_recv.at[way, g, j], (x_up, x_down)[way])

    def zx_copy(g):
        return remote(zout.at[g], zin.at[g], zx_send.at[g], zx_recv.at[g], partner)

    def project(g):
        for p, n in enumerate(pairs[g]):
            for j in range(2):
                shared(n, j).wait_recv()
            place = lax.rem(y + n, NY)
            sums = None
            for a in range(2):
                rows = wg[a, :, place].reshape(4 * ROWS, FEAT)
                more = lax.dot_general(att[a], rows, NT, preferred_element_type=jnp.float32)
                sums = more if sums is None else sums + more
            for j in range(2):
                part[g, j, :, :, :, p * TILE:(p + 1) * TILE] = sums[:, j * TILE:(j + 1) * TILE].astype(
                    jnp.bfloat16).reshape(2, NX, ROWS, TILE)
        for j in range(2):
            far_copy(g, j).start()
        for j in range(2):
            near_copy(1 - j, g, j).start()

    def pass_on(g):
        for j in range(2):
            far_copy(g, j).wait_recv()
            to = (xr, xl)[j]
            part[g, j, :, to] = (part[g, j, :, to].astype(jnp.float32) + far[g, j].astype(jnp.float32)).astype(jnp.bfloat16)
            near_copy(j, g, j).start()

    def columns(side, g, j, p):
        return pl.ds(pl.multiple_of(((side * 2 + j) * NY + lax.rem(y + pairs[g][p], NY)) * TILE, TILE), TILE)

    def finish(g):
        for j in range(2):
            for way in (1 - j, j):
                near_copy(way, g, j).wait_recv()

            def whole(b):
                return (part[g, j, b, x].astype(jnp.float32) + near[0, g, j, b].astype(jnp.float32)
                        + near[1, g, j, b].astype(jnp.float32)).astype(jnp.bfloat16)

            zout[g, j] = whole(1 - zl)
            kept = whole(zl)
            for p in range(2):
                out_ref[:, columns(zl, g, j, p)] = kept[:, p * TILE:(p + 1) * TILE]
        zx_copy(g).start()

    def place(g):
        zx_copy(g).wait_recv()
        for j in range(2):
            for p in range(2):
                out_ref[:, columns(1 - zl, g, j, p)] = zin[g, j, :, p * TILE:(p + 1) * TILE]

    project(0)
    project(1)
    pass_on(0)
    ring_step(3, 1)
    project(2)
    pass_on(1)
    ring_end()
    project(3)
    finish(0)
    pass_on(2)
    finish(1)
    pass_on(3)
    finish(2)
    place(0)
    place(1)
    finish(3)
    place(2)
    place(3)

    for condition, copies in sends.values():
        sent_if(condition, copies)
    for r in range(2):
        for j in range(1, NZ):
            z_copy(j, r).wait_send()

        @pl.when(half != zl)
        def _():
            z_copy(0, r).wait_send()

    for j in range(2):
        for n in range(UP + j):
            ring_up(n, j).wait_send()
        for n in range(DOWN + 1 - j):
            ring_down(n, j).wait_send()
        for n in range(NY):
            share(n, j).wait_send()
    for i in range(TOK // TILE):
        send_att(i).wait_send()
    for g in range(4):
        for j in range(2):
            far_copy(g, j).wait_send()
            near_copy(0, g, j).wait_send()
            near_copy(1, g, j).wait_send()
        zx_copy(g).wait_send()


def on_device(query_feats, key_feats, value_feats, span_class, ramp_width, doc_lengths, out_proj):
    bf16, f32 = jnp.bfloat16, jnp.float32
    dma = pltpu.SemaphoreType.DMA
    return pl.pallas_call(
        kernel,
        out_shape=jax.ShapeDtypeStruct((ROWS, 8 * FEAT), bf16),
        in_specs=[pl.BlockSpec(memory_space=pltpu.HBM)] * 7,
        out_specs=pl.BlockSpec(memory_space=pltpu.VMEM),
        scratch_shapes=[
            pltpu.VMEM((TOK, FEAT), bf16),
            pltpu.VMEM((TOK, HD), bf16),
            pltpu.VMEM((TOK, HD), bf16),
            pltpu.VMEM((ROWS, FEAT), bf16),
            pltpu.SMEM((32,), jnp.int32),
            pltpu.SMEM((32,), jnp.int32),
            pltpu.SMEM((NDOCS,), jnp.int32),
            pltpu.VMEM((4, TOK, HD), bf16),
            pltpu.VMEM((4, TOK, HD), bf16),
            pltpu.VMEM((4, HEADS * TILE, 2 * HD), bf16),
            pltpu.VMEM((5, TOK, HD), bf16),
            pltpu.VMEM((HEADS, 5, TILE, HD), f32),
            pltpu.VMEM((HEADS * TILE, TOK), f32),
            pltpu.VMEM((HEADS * TILE, TOK), f32),
            pltpu.VMEM((HEADS * TILE, TOK), bf16),
            pltpu.VMEM((HEADS * TILE, TOK), bf16),
            pltpu.VMEM((4, HEADS * TILE, HD), f32),
            pltpu.VMEM((4, HEADS * TILE, 2 * HD), f32),
            pltpu.VMEM((2, TOK, FEAT), bf16),
            pltpu.VMEM((2, 2, NY, 2, ROWS, FEAT), bf16),
            pltpu.VMEM((4, 2, 2, NX, ROWS, 2 * TILE), bf16),
            pltpu.VMEM((4, 2, 2, ROWS, 2 * TILE), bf16),
            pltpu.VMEM((2, 4, 2, 2, ROWS, 2 * TILE), bf16),
            pltpu.VMEM((4, 2, ROWS, 2 * TILE), bf16),
            pltpu.VMEM((4, 2, ROWS, 2 * TILE), bf16),
            pltpu.VMEM((TOK, HD), bf16), pltpu.VMEM((TOK, HD), bf16), dma((2,)), dma((2,)), dma((7,)), dma((5, 2)), dma((4, 2)), dma((NZ, 2)), dma((2, 2, 2)),
            dma((UP + 1, 2)), dma((UP + 1, 2)), dma((DOWN + 1, 2)), dma((DOWN + 1, 2)),
            dma((NY, 2)), dma((NY, 2)), dma((4,)), dma((4,)),
            dma((4, 2)), dma((4, 2)), dma((2, 4, 2)), dma((2, 4, 2)),
            dma((4,)), dma((4,)),
        ],
        compiler_params=pltpu.CompilerParams(
            collective_id=0, has_side_effects=True, vmem_limit_bytes=60 * 2**20),
        cost_estimate=pl.CostEstimate(flops=8 * 10**9, bytes_accessed=2 * 10**6, transcendentals=6 * 10**6),
        name="layer",
    )(query_feats, key_feats, value_feats, out_proj, span_class, ramp_width, doc_lengths)


def solution(mesh):
    split = P("seq", "head")
    return jax.shard_map(
        on_device, mesh=mesh, in_specs=(split, split, split, P(), P(), P(), split),
        out_specs=P(("seq", "head"), None), check_vma=False)
```

```python
import math

import jax
import jax.numpy as jnp
from jax import lax
from jax.experimental import pallas as pl
from jax.experimental.pallas import tpu as pltpu
from jax.sharding import PartitionSpec as P

HD = 128
TILE = 128
HEADS = 4
TOK = 512
FEAT = HEADS * HD
NZ, NY, NX = 4, 8, 4
NDOCS = 16
ROWS = 64
UP, DOWN = 2, 4
LOW = -1e30
MESH = pl.DeviceIdType.MESH
NT = (((1,), (1,)), ((), ()))
SCALE = math.log2(math.e) / math.sqrt(HD)


def kernel(q_hbm, k_hbm, v_hbm, w_hbm, span_hbm, ramp_hbm, doc_hbm, out_ref,
           q_ref, k_ref, v_ref, w_ref, span_ref, ramp_ref, doc_ref,
           kbuf, vbuf, qx, kf, btab, s_one, s_two, p_one, p_two, m_scr, acc, att, wg, part,
           far, near, zout, zin,
           khop, vhop, hop_send, hop_recv, in_sem, kv_send, kv_recv, z_send, z_recv, p_send, p_recv, m_send, m_recv,
           s_send, s_recv, a_send, a_recv, far_send, far_recv, near_send, near_recv,
           zx_send, zx_recv):
    loads = [pltpu.make_async_copy(src, dst, in_sem.at[n]) for n, (src, dst) in enumerate((
        (doc_hbm, doc_ref), (span_hbm, span_ref), (ramp_hbm, ramp_ref), (k_hbm, k_ref),
        (v_hbm, v_ref), (w_hbm, w_ref), (q_hbm, q_ref)))]
    for c in loads:
        c.start()
    s_scr, p_scr = (s_one, s_two), (p_one, p_two)
    seq = lax.axis_index("seq")
    head = lax.axis_index("head")
    core = lax.rem(seq, 2)
    y = lax.rem(seq // 2, NY)
    zh = seq // (2 * NY)
    x = lax.rem(head, NX)
    zl = head // NX
    half = zh // 2
    n_seq = 2 * NY * NZ
    chip = seq // 2
    last_chip = NY * NZ - 1
    leaves = zh < NZ - 1
    came = zh > 0

    def at(zh_, y_, c_, zl_, x_):
        return ((zh_ * NY + y_) * 2 + c_, zl_ * NX + x_)

    after = (lax.rem(seq + 2, n_seq), head)
    before = (lax.rem(seq + n_seq - 2, n_seq), head)
    sibling = at(zh, y, 1 - core, zl, x)
    y_up = at(zh, lax.rem(y + 1, NY), core, zl, x)
    y_down = at(zh, lax.rem(y + NY - 1, NY), core, zl, x)
    xr, xl = lax.rem(x + 1, NX), lax.rem(x + NX - 1, NX)
    xo = lax.rem(x + 2, NX)
    x_up = at(zh, y, core, zl, xr)
    x_down = at(zh, y, core, zl, xl)
    z_next = at(lax.rem(zh + 1, NZ), y, core, zl, x)
    partner = at(zh, y, core, 1 - zl, x)

    @pl.when(chip < 2)
    def _():
        kbuf[...] = jnp.zeros_like(kbuf)
        vbuf[...] = jnp.zeros_like(vbuf)

    barrier = pltpu.get_barrier_semaphore()
    greet = [sibling, y_up, y_down, x_up, x_down, partner]
    for j in range(1, NZ):
        for b in range(2):
            greet.append(at(lax.rem(zh + j, NZ), y, core, b, x))
    for device in greet:
        pl.semaphore_signal(barrier, inc=1, device_id=device, device_id_type=MESH)

    @pl.when(chip < last_chip)
    def _():
        pl.semaphore_signal(barrier, inc=1, device_id=after, device_id_type=MESH)

    @pl.when(chip > 0)
    def _():
        pl.semaphore_signal(barrier, inc=1, device_id=before, device_id_type=MESH)

    for c in loads:
        c.wait()

    pl.semaphore_wait(barrier, len(greet) + jnp.where(chip < last_chip, 1, 0) + jnp.where(chip > 0, 1, 0))

    def remote(src, dst, send, recv, device):
        return pltpu.make_async_remote_copy(
            src_ref=src, dst_ref=dst, send_sem=send, recv_sem=recv,
            device_id=device, device_id_type=MESH)

    def kv_copies(k_src, v_src, slot, n, device):
        return (remote(k_src, kbuf.at[slot], kv_send.at[n, 0], kv_recv.at[slot, 0], device),
                remote(v_src, vbuf.at[slot], kv_send.at[n, 1], kv_recv.at[slot, 1], device))

    def start(copies):
        for c in copies:
            c.start()

    def start_if(condition, copies):
        @pl.when(condition)
        def _():
            start(copies)

    def sent_if(condition, copies):
        @pl.when(condition)
        def _():
            for c in copies:
                c.wait_send()

    def kv_arrived(slot, condition):
        @pl.when(condition)
        def _():
            for c in kv_copies(k_ref, v_ref, slot, 0, sibling):
                c.wait_recv()

    k_on, v_on = kv_copies(k_ref, v_ref, 1, 0, after)
    k_aside = remote(kbuf.at[1], khop, hop_send.at[1], hop_recv.at[1], z_next)
    v_aside = remote(v_ref, vhop, hop_send.at[0], hop_recv.at[0], z_next)
    k_second, v_second = kv_copies(kbuf.at[1], vbuf.at[1], 3, 1, after)
    sends = dict(
        k_on=(chip < last_chip, (k_on,)),
        v_on=(y < NY - 1, (v_on,)),
        v_aside=((y == NY - 1) & leaves, (v_aside,)),
        v_after=((y == NY - 1) & came, kv_copies(khop, vhop, 1, 4, y_up)[1:]),
        v_second=((chip > 0) & (chip < last_chip), (v_second,)),
        k_second=((chip > 0) & (y < NY - 1), (k_second,)),
        k_aside=((y == NY - 1) & leaves, (k_aside,)),
        k_after=((y == NY - 1) & came, kv_copies(khop, vhop, 3, 4, y_up)[:1]),
        own_over=(core == 0, kv_copies(k_ref, v_ref, 0, 2, sibling)),
        first_over=((core == 1) & (chip > 0), kv_copies(kbuf.at[1], vbuf.at[1], 0, 2, sibling)),
        even_over=((core == 0) & (chip > 0), kv_copies(kbuf.at[1], vbuf.at[1], 2, 3, sibling)),
        odd_over=((core == 1) & (chip > 1), kv_copies(kbuf.at[3], vbuf.at[3], 2, 3, sibling)),
    )
    for name in ("k_on", "v_aside", "v_on", "own_over"):
        start_if(*sends[name])

    mine = (zl, lax.rem(zh, 2))

    def part_of(ref, r):
        return ref.at[pl.ds(r * (ROWS // 2), ROWS // 2)]

    def z_copy(j, r):
        target = at(lax.rem(zh + j, NZ), y, core, half, x)
        return remote(part_of(w_ref, r), part_of(wg.at[mine[0], mine[1], y, core], r), z_send.at[j, r],
                      z_recv.at[mine[0], mine[1], r], target)

    for r in range(2):
        for j in range(1, NZ):
            z_copy(j, r).start()

        @pl.when(half == zl)
        def _():
            pltpu.make_async_copy(part_of(w_ref, r), part_of(wg.at[mine[0], mine[1], y, core], r),
                                  z_recv.at[mine[0], mine[1], r]).start()

        @pl.when(half != zl)
        def _():
            z_copy(0, r).start()

    def chunk(n, j, c_):
        rows = pl.ds(pl.multiple_of(j * (ROWS // 2), ROWS // 2), ROWS // 2)
        return wg.at[:, :, lax.rem(y + n, NY), c_, rows]

    def ring_up(n, j):
        src = chunk(NY - n, j, core)
        return remote(src, src, p_send.at[n, j], p_recv.at[n, j], y_up)

    def ring_down(n, j):
        src = chunk(n, j, core)
        return remote(src, src, m_send.at[n, j], m_recv.at[n, j], y_down)

    def got_up(n, j):
        src = chunk(NY - n - 1, j, core)
        return remote(src, src, p_send.at[n, j], p_recv.at[n, j], y_up)

    def got_down(n, j):
        src = chunk(n + 1, j, core)
        return remote(src, src, m_send.at[n, j], m_recv.at[n, j], y_down)

    def share(n, j):
        src = chunk(n, j, core)
        return remote(src, src, s_send.at[n, j], s_recv.at[n, j], sibling)

    def shared(n, j):
        src = chunk(n, j, 1 - core)
        return remote(src, src, s_send.at[n, j], s_recv.at[n, j], sibling)

    def ring_begin():
        for j in range(2):
            for a in range(2):
                for b in range(2):
                    remote(part_of(w_ref, j), part_of(wg.at[a, b, y, core], j), z_send.at[0, j],
                           z_recv.at[a, b, j], sibling).wait_recv()
            ring_down(0, j).start()
            ring_up(0, j).start()
            share(0, j).start()

    def ring_step(n, j):
        def down():
            got_down(n, j).wait_recv()
            if n + 1 < DOWN:
                ring_down(n + 1, j).start()
            elif n + 1 == DOWN:
                @pl.when(j == 0)
                def _():
                    ring_down(n + 1, j).start()

            share(n + 1, j).start()

        def up():
            got_up(n, j).wait_recv()
            if n + 1 < UP:
                ring_up(n + 1, j).start()
            elif n + 1 == UP:
                @pl.when(j == 1)
                def _():
                    ring_up(n + 1, j).start()

            share(NY - n - 1, j).start()

        down()
        if n < UP:
            up()
        elif n == UP:
            pl.when(j == 1)(up)

    def ring_end():
        got_down(DOWN, 0).wait_recv()
        share(DOWN + 1, 0).start()

    lane = lax.broadcasted_iota(jnp.int32, (1, HD), 1)
    starts = jnp.zeros((1, HD), jnp.int32)
    ends = jnp.zeros((1, HD), jnp.int32)
    total = jnp.int32(0)
    for n in range(NDOCS):
        starts = jnp.where(lane == n, total, starts)
        total = total + doc_ref[n]
        ends = jnp.where(lane == n, total, ends)
    row_of = lax.broadcasted_iota(jnp.int32, (TILE, HD), 0)
    lane_of = lax.broadcasted_iota(jnp.int32, (TILE, HD), 1)
    named = lane_of < NDOCS

    def features(n, carry):
        pos = seq * TOK + n * TILE + row_of
        inside = (pos >= starts) & (pos < ends)
        other = jnp.where(named & jnp.logical_not(inside), 1.0, 0.0).astype(jnp.bfloat16)
        for h in range(HEADS):
            qx[n, h * TILE:(h + 1) * TILE, HD:] = other
            qx[n, h * TILE:(h + 1) * TILE, :HD] = q_ref[pl.ds(pl.multiple_of(n * TILE, TILE), TILE), h * HD:(h + 1) * HD]
        for d in range(5):
            key_pos = pos - d * TOK
            hidden = ((key_pos >= starts) & (key_pos < ends)) | (key_pos < 0)
            kf[d, pl.ds(pl.multiple_of(n * TILE, TILE), TILE), :] = jnp.where(named & hidden, LOW, 0.0).astype(jnp.bfloat16)
        return carry

    lax.fori_loop(0, TOK // TILE, features, 0)

    diff = (row_of - lane_of).astype(jnp.float32)

    def weight(distance_left, ramp, seen):
        w = jnp.clip(distance_left / ramp, 0.0, 1.0)
        keep = (w > 0.0) & seen
        return jnp.where(keep, jnp.log2(jnp.where(keep, w, 1.0)), LOW)

    for h in range(HEADS):
        ramp = ramp_ref[head * HEADS + h].astype(jnp.float32)
        span = span_ref[head * HEADS + h].astype(jnp.float32) * float(TILE)
        always = diff < 1000.0
        btab[h, 0] = jnp.zeros((TILE, HD), jnp.float32)
        btab[h, 1] = weight(float(TILE) - diff, ramp, always)
        btab[h, 2] = weight(-diff, ramp, always)
        btab[h, 3] = weight(span - diff, ramp, diff >= 0.0)
        btab[h, 4] = jnp.full((TILE, HD), LOW, jnp.float32)

    def send_att(i):
        rows = att.at[zl, pl.ds(pl.multiple_of(i * TILE, TILE), TILE)]
        return remote(rows, rows, a_send.at[i], a_recv.at[i], partner)

    def attend(pair, d, keys, values):
        for one in range(2):
            kx = jnp.concatenate([keys[...], kf[d]], axis=1)
            s_scr[one][...] = lax.dot_general(qx[2 * pair + one], kx, NT, preferred_element_type=jnp.float32)
        for one in range(2):
            i = 2 * pair + one
            for h in range(HEADS):
                span = span_ref[head * HEADS + h]
                rows = slice(h * TILE, (h + 1) * TILE)
                terms = []
                for t in range(4):
                    delta = 4 * d + i - t
                    over = delta - span
                    table = jnp.where(over > 0, 4, jnp.maximum(over + 2, 0))
                    table = jnp.where(delta > 0, table, jnp.where(delta == 0, 3, 4))
                    terms.append(s_scr[one][rows, t * TILE:(t + 1) * TILE] * SCALE + btab[h, table])
                top = jnp.maximum(jnp.maximum(terms[0], terms[1]), jnp.maximum(terms[2], terms[3]))
                top = jnp.broadcast_to(jnp.max(top, axis=1, keepdims=True), (TILE, HD))
                if d > 0:
                    old = m_scr[i, rows, :]
                    top = jnp.maximum(old, top)
                    ratio = jnp.exp2(old - top)
                    acc[i, rows, :] = acc[i, rows, :] * jnp.concatenate([ratio, ratio], axis=1)
                m_scr[i, rows, :] = top
                for t in range(4):
                    p_scr[one][rows, t * TILE:(t + 1) * TILE] = jnp.exp2(terms[t] - top).astype(jnp.bfloat16)
            vx = jnp.concatenate([values[...], jnp.ones((TOK, HD), jnp.bfloat16)], axis=1)
            more = jnp.dot(p_scr[one][...], vx, preferred_element_type=jnp.float32)
            acc[i] = more if d == 0 else acc[i] + more

    def over_pairs(body):
        def step(pair, carry):
            body(pair)
            return carry

        lax.fori_loop(0, 2, step, 0)

    @over_pairs
    def _(pair):
        attend(pair, 0, k_ref, v_ref)

    @pl.when((y == NY - 1) & came)
    def _():
        v_aside.wait_recv()

    start_if(*sends["v_after"])
    late = (y == 0) & came

    def relay(now):
        kv_arrived(1, now & (chip > 0))
        for name in ("k_aside", "v_second", "k_second", "even_over", "first_over"):
            start_if(now & sends[name][0], sends[name][1])

    relay(jnp.logical_not(late))
    ring_begin()
    relay(late)

    @over_pairs
    def _(pair):
        attend(pair, 2, kbuf.at[1], vbuf.at[1])

        @pl.when((pair == 1) & (y == NY - 1) & came)
        def _():
            k_aside.wait_recv()
            sends["k_after"][1][0].start()

        ring_step(0, pair)

    kv_arrived(0, (core == 1) | (chip > 0))

    @over_pairs
    def _(pair):
        attend(pair, 1, kbuf.at[0], vbuf.at[0])

    ring_step(1, 0)

    behind = (y < 2) & came
    kv_arrived(3, chip > 1)
    start_if(*sends["odd_over"])
    kv_arrived(2, (chip > 1) | ((core == 1) & (chip > 0)))

    @over_pairs
    def _(pair):
        attend(pair, 4, kbuf.at[3], vbuf.at[3])
        attend(pair, 3, kbuf.at[2], vbuf.at[2])
        for one in range(2):
            i = 2 * pair + one
            for h in range(HEADS):
                rows = slice(h * TILE, (h + 1) * TILE)
                out = acc[i, rows, :HD] / acc[i, rows, HD:]
                att[zl, pl.ds(pl.multiple_of(i * TILE, TILE), TILE), h * HD:(h + 1) * HD] = out.astype(jnp.bfloat16)
            send_att(i).start()

        @pl.when((pair == 0) & jnp.logical_not(behind))
        def _():
            ring_step(1, 1)

    @pl.when(behind)
    def _():
        ring_step(1, 1)

    ring_step(2, 0)
    ring_step(2, 1)
    ring_step(3, 0)

    for i in range(TOK // TILE):
        rows = att.at[1 - zl, pl.ds(i * TILE, TILE)]
        remote(rows, rows, a_send.at[i], a_recv.at[i], partner).wait_recv()

    pairs = ((0, 1), (7, 2), (6, 3), (4, 5))

    def far_copy(g, j):
        return remote(part.at[g, j, :, xo], far.at[g, j], far_send.at[g, j], far_recv.at[g, j], (x_up, x_down)[j])

    def near_copy(way, g, j):
        return remote(part.at[g, j, :, (xr, xl)[way]], near.at[way, g, j], near_send.at[way, g, j],
                      near_recv.at[way, g, j], (x_up, x_down)[way])

    def zx_copy(g):
        return remote(zout.at[g], zin.at[g], zx_send.at[g], zx_recv.at[g], partner)

    def project(g):
        for p, n in enumerate(pairs[g]):
            for j in range(2):
                shared(n, j).wait_recv()
            place = lax.rem(y + n, NY)
            sums = None
            for a in range(2):
                rows = wg[a, :, place].reshape(4 * ROWS, FEAT)
                more = lax.dot_general(att[a], rows, NT, preferred_element_type=jnp.float32)
                sums = more if sums is None else sums + more
            for j in range(2):
                part[g, j, :, :, :, p * TILE:(p + 1) * TILE] = sums[:, j * TILE:(j + 1) * TILE].astype(
                    jnp.bfloat16).reshape(2, NX, ROWS, TILE)
        for j in range(2):
            far_copy(g, j).start()
        for j in range(2):
            near_copy(1 - j, g, j).start()

    def pass_on(g):
        for j in range(2):
            far_copy(g, j).wait_recv()
            to = (xr, xl)[j]
            part[g, j, :, to] = (part[g, j, :, to].astype(jnp.float32) + far[g, j].astype(jnp.float32)).astype(jnp.bfloat16)
            near_copy(j, g, j).start()

    def columns(side, g, j, p):
        return pl.ds(pl.multiple_of(((side * 2 + j) * NY + lax.rem(y + pairs[g][p], NY)) * TILE, TILE), TILE)

    def finish(g):
        for j in range(2):
            for way in (1 - j, j):
                near_copy(way, g, j).wait_recv()

            def whole(b):
                return (part[g, j, b, x].astype(jnp.float32) + near[0, g, j, b].astype(jnp.float32)
                        + near[1, g, j, b].astype(jnp.float32)).astype(jnp.bfloat16)

            zout[g, j] = whole(1 - zl)
            kept = whole(zl)
            for p in range(2):
                out_ref[:, columns(zl, g, j, p)] = kept[:, p * TILE:(p + 1) * TILE]
        zx_copy(g).start()

    def place(g):
        zx_copy(g).wait_recv()
        for j in range(2):
            for p in range(2):
                out_ref[:, columns(1 - zl, g, j, p)] = zin[g, j, :, p * TILE:(p + 1) * TILE]

    project(0)
    project(1)
    pass_on(0)
    ring_step(3, 1)
    project(2)
    pass_on(1)
    ring_end()
    project(3)
    finish(0)
    pass_on(2)
    finish(1)
    pass_on(3)
    finish(2)
    place(0)
    place(1)
    finish(3)
    place(2)
    place(3)

    for condition, copies in sends.values():
        sent_if(condition, copies)
    for r in range(2):
        for j in range(1, NZ):
            z_copy(j, r).wait_send()

        @pl.when(half != zl)
        def _():
            z_copy(0, r).wait_send()

    for j in range(2):
        for n in range(UP + j):
            ring_up(n, j).wait_send()
        for n in range(DOWN + 1 - j):
            ring_down(n, j).wait_send()
        for n in range(NY):
            share(n, j).wait_send()
    for i in range(TOK // TILE):
        send_att(i).wait_send()
    for g in range(4):
        for j in range(2):
            far_copy(g, j).wait_send()
            near_copy(0, g, j).wait_send()
            near_copy(1, g, j).wait_send()
        zx_copy(g).wait_send()


def on_device(query_feats, key_feats, value_feats, span_class, ramp_width, doc_lengths, out_proj):
    bf16, f32 = jnp.bfloat16, jnp.float32
    dma = pltpu.SemaphoreType.DMA
    return pl.pallas_call(
        kernel,
        out_shape=jax.ShapeDtypeStruct((ROWS, 8 * FEAT), bf16),
        in_specs=[pl.BlockSpec(memory_space=pltpu.HBM)] * 7,
        out_specs=pl.BlockSpec(memory_space=pltpu.VMEM),
        scratch_shapes=[
            pltpu.VMEM((TOK, FEAT), bf16),
            pltpu.VMEM((TOK, HD), bf16),
            pltpu.VMEM((TOK, HD), bf16),
            pltpu.VMEM((ROWS, FEAT), bf16),
            pltpu.SMEM((32,), jnp.int32),
            pltpu.SMEM((32,), jnp.int32),
            pltpu.SMEM((NDOCS,), jnp.int32),
            pltpu.VMEM((4, TOK, HD), bf16),
            pltpu.VMEM((4, TOK, HD), bf16),
            pltpu.VMEM((4, HEADS * TILE, 2 * HD), bf16),
            pltpu.VMEM((5, TOK, HD), bf16),
            pltpu.VMEM((HEADS, 5, TILE, HD), f32),
            pltpu.VMEM((HEADS * TILE, TOK), f32),
            pltpu.VMEM((HEADS * TILE, TOK), f32),
            pltpu.VMEM((HEADS * TILE, TOK), bf16),
            pltpu.VMEM((HEADS * TILE, TOK), bf16),
            pltpu.VMEM((4, HEADS * TILE, HD), f32),
            pltpu.VMEM((4, HEADS * TILE, 2 * HD), f32),
            pltpu.VMEM((2, TOK, FEAT), bf16),
            pltpu.VMEM((2, 2, NY, 2, ROWS, FEAT), bf16),
            pltpu.VMEM((4, 2, 2, NX, ROWS, 2 * TILE), bf16),
            pltpu.VMEM((4, 2, 2, ROWS, 2 * TILE), bf16),
            pltpu.VMEM((2, 4, 2, 2, ROWS, 2 * TILE), bf16),
            pltpu.VMEM((4, 2, ROWS, 2 * TILE), bf16),
            pltpu.VMEM((4, 2, ROWS, 2 * TILE), bf16),
            pltpu.VMEM((TOK, HD), bf16), pltpu.VMEM((TOK, HD), bf16), dma((2,)), dma((2,)), dma((7,)), dma((5, 2)), dma((4, 2)), dma((NZ, 2)), dma((2, 2, 2)),
            dma((UP + 1, 2)), dma((UP + 1, 2)), dma((DOWN + 1, 2)), dma((DOWN + 1, 2)),
            dma((NY, 2)), dma((NY, 2)), dma((4,)), dma((4,)),
            dma((4, 2)), dma((4, 2)), dma((2, 4, 2)), dma((2, 4, 2)),
            dma((4,)), dma((4,)),
        ],
        compiler_params=pltpu.CompilerParams(
            collective_id=0, has_side_effects=True, vmem_limit_bytes=60 * 2**20),
        cost_estimate=pl.CostEstimate(flops=8 * 10**9, bytes_accessed=2 * 10**6, transcendentals=6 * 10**6),
        name="layer",
    )(query_feats, key_feats, value_feats, out_proj, span_class, ramp_width, doc_lengths)


def solution(mesh):
    split = P("seq", "head")
    return jax.shard_map(
        on_device, mesh=mesh, in_specs=(split, split, split, P(), P(), P(), split),
        out_specs=P(("seq", "head"), None), check_vma=False)
```

```python
import math

import jax
import jax.numpy as jnp
from jax import lax
from jax.experimental import pallas as pl
from jax.experimental.pallas import tpu as pltpu
from jax.sharding import PartitionSpec as P

HD = 128
TILE = 128
HEADS = 4
TOK = 512
FEAT = HEADS * HD
NZ, NY, NX = 4, 8, 4
NDOCS = 16
ROWS = 64
UP, DOWN = 2, 4
LOW = -1e30
MESH = pl.DeviceIdType.MESH
NT = (((1,), (1,)), ((), ()))
SCALE = math.log2(math.e) / math.sqrt(HD)


def kernel(q_hbm, k_hbm, v_hbm, w_hbm, span_hbm, ramp_hbm, doc_hbm, out_ref,
           q_ref, k_ref, v_ref, w_ref, span_ref, ramp_ref, doc_ref,
           kbuf, vbuf, qx, kf, btab, s_one, s_two, p_one, p_two, m_scr, acc, att, wg, part,
           far, near, zout, zin,
           khop, vhop, hop_send, hop_recv, in_sem, kv_send, kv_recv, z_send, z_recv, p_send, p_recv, m_send, m_recv,
           s_send, s_recv, a_send, a_recv, far_send, far_recv, near_send, near_recv,
           zx_send, zx_recv):
    loads = [pltpu.make_async_copy(src, dst, in_sem.at[n]) for n, (src, dst) in enumerate((
        (doc_hbm, doc_ref), (span_hbm, span_ref), (ramp_hbm, ramp_ref), (k_hbm, k_ref),
        (v_hbm, v_ref), (w_hbm, w_ref), (q_hbm, q_ref)))]
    for c in loads:
        c.start()
    s_scr, p_scr = (s_one, s_two), (p_one, p_two)
    seq = lax.axis_index("seq")
    head = lax.axis_index("head")
    core = lax.rem(seq, 2)
    y = lax.rem(seq // 2, NY)
    zh = seq // (2 * NY)
    x = lax.rem(head, NX)
    zl = head // NX
    half = zh // 2
    n_seq = 2 * NY * NZ
    chip = seq // 2
    last_chip = NY * NZ - 1
    leaves = zh < NZ - 1
    came = zh > 0

    def at(zh_, y_, c_, zl_, x_):
        return ((zh_ * NY + y_) * 2 + c_, zl_ * NX + x_)

    after = (lax.rem(seq + 2, n_seq), head)
    before = (lax.rem(seq + n_seq - 2, n_seq), head)
    sibling = at(zh, y, 1 - core, zl, x)
    y_up = at(zh, lax.rem(y + 1, NY), core, zl, x)
    y_down = at(zh, lax.rem(y + NY - 1, NY), core, zl, x)
    xr, xl = lax.rem(x + 1, NX), lax.rem(x + NX - 1, NX)
    xo = lax.rem(x + 2, NX)
    x_up = at(zh, y, core, zl, xr)
    x_down = at(zh, y, core, zl, xl)
    z_next = at(lax.rem(zh + 1, NZ), y, core, zl, x)
    partner = at(zh, y, core, 1 - zl, x)

    @pl.when(chip < 2)
    def _():
        kbuf[...] = jnp.zeros_like(kbuf)
        vbuf[...] = jnp.zeros_like(vbuf)

    barrier = pltpu.get_barrier_semaphore()
    greet = [sibling, y_up, y_down, x_up, x_down, partner]
    for j in range(1, NZ):
        for b in range(2):
            greet.append(at(lax.rem(zh + j, NZ), y, core, b, x))
    for device in greet:
        pl.semaphore_signal(barrier, inc=1, device_id=device, device_id_type=MESH)

    @pl.when(chip < last_chip)
    def _():
        pl.semaphore_signal(barrier, inc=1, device_id=after, device_id_type=MESH)

    @pl.when(chip > 0)
    def _():
        pl.semaphore_signal(barrier, inc=1, device_id=before, device_id_type=MESH)

    for c in loads:
        c.wait()

    pl.semaphore_wait(barrier, len(greet) + jnp.where(chip < last_chip, 1, 0) + jnp.where(chip > 0, 1, 0))

    def remote(src, dst, send, recv, device):
        return pltpu.make_async_remote_copy(
            src_ref=src, dst_ref=dst, send_sem=send, recv_sem=recv,
            device_id=device, device_id_type=MESH)

    def kv_copies(k_src, v_src, slot, n, device):
        return (remote(k_src, kbuf.at[slot], kv_send.at[n, 0], kv_recv.at[slot, 0], device),
                remote(v_src, vbuf.at[slot], kv_send.at[n, 1], kv_recv.at[slot, 1], device))

    def start(copies):
        for c in copies:
            c.start()

    def start_if(condition, copies):
        @pl.when(condition)
        def _():
            start(copies)

    def sent_if(condition, copies):
        @pl.when(condition)
        def _():
            for c in copies:
                c.wait_send()

    def kv_arrived(slot, condition):
        @pl.when(condition)
        def _():
            for c in kv_copies(k_ref, v_ref, slot, 0, sibling):
                c.wait_recv()

    k_on, v_on = kv_copies(k_ref, v_ref, 1, 0, after)
    k_aside = remote(kbuf.at[1], khop, hop_send.at[1], hop_recv.at[1], z_next)
    v_aside = remote(v_ref, vhop, hop_send.at[0], hop_recv.at[0], z_next)
    k_second, v_second = kv_copies(kbuf.at[1], vbuf.at[1], 3, 1, after)
    sends = dict(
        k_on=(chip < last_chip, (k_on,)),
        v_on=(y < NY - 1, (v_on,)),
        v_aside=((y == NY - 1) & leaves, (v_aside,)),
        v_after=((y == NY - 1) & came, kv_copies(khop, vhop, 1, 4, y_up)[1:]),
        v_second=((chip > 0) & (chip < last_chip), (v_second,)),
        k_second=((chip > 0) & (y < NY - 1), (k_second,)),
        k_aside=((y == NY - 1) & leaves, (k_aside,)),
        k_after=((y == NY - 1) & came, kv_copies(khop, vhop, 3, 4, y_up)[:1]),
        own_over=(core == 0, kv_copies(k_ref, v_ref, 0, 2, sibling)),
        first_over=((core == 1) & (chip > 0), kv_copies(kbuf.at[1], vbuf.at[1], 0, 2, sibling)),
        even_over=((core == 0) & (chip > 0), kv_copies(kbuf.at[1], vbuf.at[1], 2, 3, sibling)),
        odd_over=((core == 1) & (chip > 1), kv_copies(kbuf.at[3], vbuf.at[3], 2, 3, sibling)),
    )
    for name in ("k_on", "v_aside", "v_on", "own_over"):
        start_if(*sends[name])

    mine = (zl, lax.rem(zh, 2))

    def part_of(ref, r):
        return ref.at[pl.ds(r * (ROWS // 2), ROWS // 2)]

    def z_copy(j, r):
        target = at(lax.rem(zh + j, NZ), y, core, half, x)
        return remote(part_of(w_ref, r), part_of(wg.at[mine[0], mine[1], y, core], r), z_send.at[j, r],
                      z_recv.at[mine[0], mine[1], r], target)

    for r in range(2):
        for j in range(1, NZ):
            z_copy(j, r).start()

        @pl.when(half == zl)
        def _():
            pltpu.make_async_copy(part_of(w_ref, r), part_of(wg.at[mine[0], mine[1], y, core], r),
                                  z_recv.at[mine[0], mine[1], r]).start()

        @pl.when(half != zl)
        def _():
            z_copy(0, r).start()

    def chunk(n, j, c_):
        rows = pl.ds(pl.multiple_of(j * (ROWS // 2), ROWS // 2), ROWS // 2)
        return wg.at[:, :, lax.rem(y + n, NY), c_, rows]

    def ring_up(n, j):
        src = chunk(NY - n, j, core)
        return remote(src, src, p_send.at[n, j], p_recv.at[n, j], y_up)

    def ring_down(n, j):
        src = chunk(n, j, core)
        return remote(src, src, m_send.at[n, j], m_recv.at[n, j], y_down)

    def got_up(n, j):
        src = chunk(NY - n - 1, j, core)
        return remote(src, src, p_send.at[n, j], p_recv.at[n, j], y_up)

    def got_down(n, j):
        src = chunk(n + 1, j, core)
        return remote(src, src, m_send.at[n, j], m_recv.at[n, j], y_down)

    def share(n, j):
        src = chunk(n, j, core)
        return remote(src, src, s_send.at[n, j], s_recv.at[n, j], sibling)

    def shared(n, j):
        src = chunk(n, j, 1 - core)
        return remote(src, src, s_send.at[n, j], s_recv.at[n, j], sibling)

    def ring_begin():
        for j in range(2):
            for a in range(2):
                for b in range(2):
                    remote(part_of(w_ref, j), part_of(wg.at[a, b, y, core], j), z_send.at[0, j],
                           z_recv.at[a, b, j], sibling).wait_recv()
            ring_down(0, j).start()
            ring_up(0, j).start()
            share(0, j).start()

    def ring_step(n, j):
        def down():
            got_down(n, j).wait_recv()
            if n + 1 < DOWN:
                ring_down(n + 1, j).start()
            elif n + 1 == DOWN:
                @pl.when(j == 0)
                def _():
                    ring_down(n + 1, j).start()

            share(n + 1, j).start()

        def up():
            got_up(n, j).wait_recv()
            if n + 1 < UP:
                ring_up(n + 1, j).start()
            elif n + 1 == UP:
                @pl.when(j == 1)
                def _():
                    ring_up(n + 1, j).start()

            share(NY - n - 1, j).start()

        down()
        if n < UP:
            up()
        elif n == UP:
            pl.when(j == 1)(up)

    def ring_end():
        got_down(DOWN, 0).wait_recv()
        share(DOWN + 1, 0).start()

    lane = lax.broadcasted_iota(jnp.int32, (1, HD), 1)
    starts = jnp.zeros((1, HD), jnp.int32)
    ends = jnp.zeros((1, HD), jnp.int32)
    total = jnp.int32(0)
    for n in range(NDOCS):
        starts = jnp.where(lane == n, total, starts)
        total = total + doc_ref[n]
        ends = jnp.where(lane == n, total, ends)
    row_of = lax.broadcasted_iota(jnp.int32, (TILE, HD), 0)
    lane_of = lax.broadcasted_iota(jnp.int32, (TILE, HD), 1)
    named = lane_of < NDOCS

    def features(n, carry):
        pos = seq * TOK + n * TILE + row_of
        inside = (pos >= starts) & (pos < ends)
        other = jnp.where(named & jnp.logical_not(inside), 1.0, 0.0).astype(jnp.bfloat16)
        for h in range(HEADS):
            qx[n, h * TILE:(h + 1) * TILE, HD:] = other
            qx[n, h * TILE:(h + 1) * TILE, :HD] = q_ref[pl.ds(pl.multiple_of(n * TILE, TILE), TILE), h * HD:(h + 1) * HD]
        for d in range(5):
            key_pos = pos - d * TOK
            hidden = ((key_pos >= starts) & (key_pos < ends)) | (key_pos < 0)
            kf[d, pl.ds(pl.multiple_of(n * TILE, TILE), TILE), :] = jnp.where(named & hidden, LOW, 0.0).astype(jnp.bfloat16)
        return carry

    lax.fori_loop(0, TOK // TILE, features, 0)

    diff = (row_of - lane_of).astype(jnp.float32)

    def weight(distance_left, ramp, seen):
        w = jnp.clip(distance_left / ramp, 0.0, 1.0)
        keep = (w > 0.0) & seen
        return jnp.where(keep, jnp.log2(jnp.where(keep, w, 1.0)), LOW)

    for h in range(HEADS):
        ramp = ramp_ref[head * HEADS + h].astype(jnp.float32)
        span = span_ref[head * HEADS + h].astype(jnp.float32) * float(TILE)
        always = diff < 1000.0
        btab[h, 0] = jnp.zeros((TILE, HD), jnp.float32)
        btab[h, 1] = weight(float(TILE) - diff, ramp, always)
        btab[h, 2] = weight(-diff, ramp, always)
        btab[h, 3] = weight(span - diff, ramp, diff >= 0.0)
        btab[h, 4] = jnp.full((TILE, HD), LOW, jnp.float32)

    def send_att(i):
        rows = att.at[zl, pl.ds(pl.multiple_of(i * TILE, TILE), TILE)]
        return remote(rows, rows, a_send.at[i], a_recv.at[i], partner)

    def attend(pair, d, keys, values):
        for one in range(2):
            kx = jnp.concatenate([keys[...], kf[d]], axis=1)
            s_scr[one][...] = lax.dot_general(qx[2 * pair + one], kx, NT, preferred_element_type=jnp.float32)
        for one in range(2):
            i = 2 * pair + one
            for h in range(HEADS):
                span = span_ref[head * HEADS + h]
                rows = slice(h * TILE, (h + 1) * TILE)
                terms = []
                for t in range(4):
                    delta = 4 * d + i - t
                    over = delta - span
                    table = jnp.where(over > 0, 4, jnp.maximum(over + 2, 0))
                    table = jnp.where(delta > 0, table, jnp.where(delta == 0, 3, 4))
                    terms.append(s_scr[one][rows, t * TILE:(t + 1) * TILE] * SCALE + btab[h, table])
                top = jnp.maximum(jnp.maximum(terms[0], terms[1]), jnp.maximum(terms[2], terms[3]))
                top = jnp.broadcast_to(jnp.max(top, axis=1, keepdims=True), (TILE, HD))
                if d > 0:
                    old = m_scr[i, rows, :]
                    top = jnp.maximum(old, top)
                    ratio = jnp.exp2(old - top)
                    acc[i, rows, :] = acc[i, rows, :] * jnp.concatenate([ratio, ratio], axis=1)
                m_scr[i, rows, :] = top
                for t in range(4):
                    p_scr[one][rows, t * TILE:(t + 1) * TILE] = jnp.exp2(terms[t] - top).astype(jnp.bfloat16)
            vx = jnp.concatenate([values[...], jnp.ones((TOK, HD), jnp.bfloat16)], axis=1)
            more = jnp.dot(p_scr[one][...], vx, preferred_element_type=jnp.float32)
            acc[i] = more if d == 0 else acc[i] + more

    def over_pairs(body):
        def step(pair, carry):
            body(pair)
            return carry

        lax.fori_loop(0, 2, step, 0)

    @over_pairs
    def _(pair):
        attend(pair, 0, k_ref, v_ref)

    @pl.when((y == NY - 1) & came)
    def _():
        v_aside.wait_recv()

    start_if(*sends["v_after"])
    late = (y == 0) & came

    def relay(now):
        kv_arrived(1, now & (chip > 0))
        for name in ("k_aside", "v_second", "k_second", "even_over", "first_over"):
            start_if(now & sends[name][0], sends[name][1])

    relay(jnp.logical_not(late))
    ring_begin()
    relay(late)

    @over_pairs
    def _(pair):
        attend(pair, 2, kbuf.at[1], vbuf.at[1])

        @pl.when((pair == 1) & (y == NY - 1) & came)
        def _():
            k_aside.wait_recv()
            sends["k_after"][1][0].start()

        ring_step(0, pair)

    kv_arrived(0, (core == 1) | (chip > 0))

    @over_pairs
    def _(pair):
        attend(pair, 1, kbuf.at[0], vbuf.at[0])

    ring_step(1, 0)
    kv_arrived(3, chip > 1)
    start_if(*sends["odd_over"])
    kv_arrived(2, (chip > 1) | ((core == 1) & (chip > 0)))

    @over_pairs
    def _(pair):
        attend(pair, 4, kbuf.at[3], vbuf.at[3])
        attend(pair, 3, kbuf.at[2], vbuf.at[2])
        for one in range(2):
            i = 2 * pair + one
            for h in range(HEADS):
                rows = slice(h * TILE, (h + 1) * TILE)
                out = acc[i, rows, :HD] / acc[i, rows, HD:]
                att[zl, pl.ds(pl.multiple_of(i * TILE, TILE), TILE), h * HD:(h + 1) * HD] = out.astype(jnp.bfloat16)
            send_att(i).start()

        @pl.when(pair == 0)
        def _():
            ring_step(1, 1)

    ring_step(2, 0)
    ring_step(2, 1)
    ring_step(3, 0)

    for i in range(TOK // TILE):
        rows = att.at[1 - zl, pl.ds(i * TILE, TILE)]
        remote(rows, rows, a_send.at[i], a_recv.at[i], partner).wait_recv()

    pairs = ((0, 1), (7, 2), (6, 3), (4, 5))

    def far_copy(g, j):
        return remote(part.at[g, j, :, xo], far.at[g, j], far_send.at[g, j], far_recv.at[g, j], (x_up, x_down)[j])

    def near_copy(way, g, j):
        return remote(part.at[g, j, :, (xr, xl)[way]], near.at[way, g, j], near_send.at[way, g, j],
                      near_recv.at[way, g, j], (x_up, x_down)[way])

    def zx_copy(g):
        return remote(zout.at[g], zin.at[g], zx_send.at[g], zx_recv.at[g], partner)

    def project(g):
        for p, n in enumerate(pairs[g]):
            for j in range(2):
                shared(n, j).wait_recv()
            place = lax.rem(y + n, NY)
            sums = None
            for a in range(2):
                rows = wg[a, :, place].reshape(4 * ROWS, FEAT)
                more = lax.dot_general(att[a], rows, NT, preferred_element_type=jnp.float32)
                sums = more if sums is None else sums + more
            for j in range(2):
                part[g, j, :, :, :, p * TILE:(p + 1) * TILE] = sums[:, j * TILE:(j + 1) * TILE].astype(
                    jnp.bfloat16).reshape(2, NX, ROWS, TILE)
        for j in range(2):
            far_copy(g, j).start()

    def send_near(g):
        for j in range(2):
            near_copy(1 - j, g, j).start()

    def pass_on(g):
        for j in range(2):
            far_copy(g, j).wait_recv()
            to = (xr, xl)[j]
            part[g, j, :, to] = (part[g, j, :, to].astype(jnp.float32) + far[g, j].astype(jnp.float32)).astype(jnp.bfloat16)
            near_copy(j, g, j).start()

    def columns(side, g, j, p):
        return pl.ds(pl.multiple_of(((side * 2 + j) * NY + lax.rem(y + pairs[g][p], NY)) * TILE, TILE), TILE)

    def finish(g):
        for j in range(2):
            for way in (1 - j, j):
                near_copy(way, g, j).wait_recv()

            def whole(b):
                return (part[g, j, b, x].astype(jnp.float32) + near[0, g, j, b].astype(jnp.float32)
                        + near[1, g, j, b].astype(jnp.float32)).astype(jnp.bfloat16)

            zout[g, j] = whole(1 - zl)
            kept = whole(zl)
            for p in range(2):
                out_ref[:, columns(zl, g, j, p)] = kept[:, p * TILE:(p + 1) * TILE]
        zx_copy(g).start()

    def place(g):
        zx_copy(g).wait_recv()
        for j in range(2):
            for p in range(2):
                out_ref[:, columns(1 - zl, g, j, p)] = zin[g, j, :, p * TILE:(p + 1) * TILE]

    project(0)
    project(1)
    send_near(0)
    pass_on(0)
    ring_step(3, 1)
    project(2)
    pass_on(1)
    send_near(1)
    ring_end()
    project(3)
    pass_on(2)
    send_near(2)
    finish(0)
    pass_on(3)
    send_near(3)
    finish(1)
    finish(2)
    place(0)
    place(1)
    finish(3)
    place(2)
    place(3)

    for condition, copies in sends.values():
        sent_if(condition, copies)
    for r in range(2):
        for j in range(1, NZ):
            z_copy(j, r).wait_send()

        @pl.when(half != zl)
        def _():
            z_copy(0, r).wait_send()

    for j in range(2):
        for n in range(UP + j):
            ring_up(n, j).wait_send()
        for n in range(DOWN + 1 - j):
            ring_down(n, j).wait_send()
        for n in range(NY):
            share(n, j).wait_send()
    for i in range(TOK // TILE):
        send_att(i).wait_send()
    for g in range(4):
        for j in range(2):
            far_copy(g, j).wait_send()
            near_copy(0, g, j).wait_send()
            near_copy(1, g, j).wait_send()
        zx_copy(g).wait_send()


def on_device(query_feats, key_feats, value_feats, span_class, ramp_width, doc_lengths, out_proj):
    bf16, f32 = jnp.bfloat16, jnp.float32
    dma = pltpu.SemaphoreType.DMA
    return pl.pallas_call(
        kernel,
        out_shape=jax.ShapeDtypeStruct((ROWS, 8 * FEAT), bf16),
        in_specs=[pl.BlockSpec(memory_space=pltpu.HBM)] * 7,
        out_specs=pl.BlockSpec(memory_space=pltpu.VMEM),
        scratch_shapes=[
            pltpu.VMEM((TOK, FEAT), bf16),
            pltpu.VMEM((TOK, HD), bf16),
            pltpu.VMEM((TOK, HD), bf16),
            pltpu.VMEM((ROWS, FEAT), bf16),
            pltpu.SMEM((32,), jnp.int32),
            pltpu.SMEM((32,), jnp.int32),
            pltpu.SMEM((NDOCS,), jnp.int32),
            pltpu.VMEM((4, TOK, HD), bf16),
            pltpu.VMEM((4, TOK, HD), bf16),
            pltpu.VMEM((4, HEADS * TILE, 2 * HD), bf16),
            pltpu.VMEM((5, TOK, HD), bf16),
            pltpu.VMEM((HEADS, 5, TILE, HD), f32),
            pltpu.VMEM((HEADS * TILE, TOK), f32),
            pltpu.VMEM((HEADS * TILE, TOK), f32),
            pltpu.VMEM((HEADS * TILE, TOK), bf16),
            pltpu.VMEM((HEADS * TILE, TOK), bf16),
            pltpu.VMEM((4, HEADS * TILE, HD), f32),
            pltpu.VMEM((4, HEADS * TILE, 2 * HD), f32),
            pltpu.VMEM((2, TOK, FEAT), bf16),
            pltpu.VMEM((2, 2, NY, 2, ROWS, FEAT), bf16),
            pltpu.VMEM((4, 2, 2, NX, ROWS, 2 * TILE), bf16),
            pltpu.VMEM((4, 2, 2, ROWS, 2 * TILE), bf16),
            pltpu.VMEM((2, 4, 2, 2, ROWS, 2 * TILE), bf16),
            pltpu.VMEM((4, 2, ROWS, 2 * TILE), bf16),
            pltpu.VMEM((4, 2, ROWS, 2 * TILE), bf16),
            pltpu.VMEM((TOK, HD), bf16), pltpu.VMEM((TOK, HD), bf16), dma((2,)), dma((2,)), dma((7,)), dma((5, 2)), dma((4, 2)), dma((NZ, 2)), dma((2, 2, 2)),
            dma((UP + 1, 2)), dma((UP + 1, 2)), dma((DOWN + 1, 2)), dma((DOWN + 1, 2)),
            dma((NY, 2)), dma((NY, 2)), dma((4,)), dma((4,)),
            dma((4, 2)), dma((4, 2)), dma((2, 4, 2)), dma((2, 4, 2)),
            dma((4,)), dma((4,)),
        ],
        compiler_params=pltpu.CompilerParams(
            collective_id=0, has_side_effects=True, vmem_limit_bytes=60 * 2**20),
        cost_estimate=pl.CostEstimate(flops=8 * 10**9, bytes_accessed=2 * 10**6, transcendentals=6 * 10**6),
        name="layer",
    )(query_feats, key_feats, value_feats, out_proj, span_class, ramp_width, doc_lengths)


def solution(mesh):
    split = P("seq", "head")
    return jax.shard_map(
        on_device, mesh=mesh, in_specs=(split, split, split, P(), P(), P(), split),
        out_specs=P(("seq", "head"), None), check_vma=False)
```
